128 devices in a mesh: dp: 16 (over y_hi, z, core), tensor: 8 (over y_lo, x).
Axes of the slice: x: 4, y: 4 (y_hi: 2, y_lo: 2; y = y_hi * 2 + y_lo), z: 4, core: 2. Of those that a mesh axis runs over, the one named last changes fastest.
Arguments:
- weight: float32 [1024, 15872], P(None, 'tensor'), may hold values from -3 to 3
- grad_parts: float32 [16, 1024, 15872], P('dp', None, 'tensor'), may hold values from -6 to 6
- m_codes: int32 [7936, 2048], P(('dp', 'tensor')), may hold values from 0 to 255
- v_codes: int32 [7936, 2048], P(('dp', 'tensor')), may hold values from 0 to 255
- m_absmax: float32 [7936], P(('dp', 'tensor')), may hold values from 0.1 to 1
- v_absmax: float32 [7936], P(('dp', 'tensor')), may hold values from 0.001 to 0.01
- code_m: float32 [256], replicated, may hold values from -1 to 1
- code_v: float32 [256], replicated, may hold values from 0.05 to 1
- step: int32 [1], replicated, may hold values from 1 to 64
Outputs:
- new_weight: float32 [1024, 15872], P(None, 'tensor')
- m_scaled: bfloat16 [7936, 2048], P(('dp', 'tensor'))
- v_scaled: bfloat16 [7936, 2048], P(('dp', 'tensor'))
- m_absmax_new: float32 [7936], P(('dp', 'tensor'))
- v_absmax_new: float32 [7936], P(('dp', 'tensor'))
The draws below stay inside these ranges and needn't reach their ends.
All inputs are finite; a program needn't handle non-finite values. Where the reference program divides by a largest or mean magnitude, that divisor is 1e-20 or more.
Results may differ from the reference program's by a relative error of at most 0.001.
Values sent between devices are 32-bit elements; how exact they have to be, the bound alone decides.
No kernel may reach another device: no remote copies, remote signals or barrier semaphores. Data moves between devices by JAX's collectives and lax.ppermute only.
A program may use at most 128 MiB of HBM per device.

```python
import math
import jax
import jax.numpy as jnp
from jax import lax

QKV = 15872
BLOCK = 2048
CODES = 256
ROWS = 1024
NBLK = 7936
N_DP = 16


def plant(result, own_key, low, high):
    longest = result.shape.index(max(result.shape))
    spots = []
    for shift in (0, 1):
        where = [jax.random.randint(jax.random.fold_in(own_key, axis), (), 0, length) for axis, length in enumerate(result.shape)]
        where[longest] = (where[longest] + shift) % result.shape[longest]
        spots.append(tuple(where))
    return result.at[spots[0]].set(low).at[spots[1]].set(high)


def with_spikes(entries, rng, source, target, parts, factor):
    owner, partner = [(jnp.arange(entries.shape[position]) // (entries.shape[position] // parts)).reshape([-1 if axis == position else 1 for axis in range(entries.ndim)]) for position in (source, target)]
    chosen = jax.random.permutation(rng, parts)[partner]
    strong = (owner == chosen) | (owner == (partner + parts // 2) % parts)
    return jnp.where(strong, factor * entries, entries)


def block_scale(key, shape, shards, least, largest):
    loudness = 1.0
    for position, blocks in shards:
        draws = jax.random.uniform(jax.random.fold_in(jax.random.fold_in(key, 6), position), (blocks,), jnp.float32, least / len(shards), largest / len(shards))
        loudness = loudness * jnp.repeat(jnp.exp(draws), shape[position] // blocks).reshape((-1,) + (1,) * (len(shape) - 1 - position))
    return loudness


def normal_values(rng, dims, deviation, bound, split=(), held_as=jnp.bfloat16):
    level = block_scale(rng, dims, split, -0.22, 0.18) if split else 1.0
    values = jax.random.normal(rng, dims, jnp.float32) * deviation * level
    return jnp.minimum(jnp.maximum(values, -bound), bound).astype(held_as)


def bell_draw_with(stream_key, extent, spread, limit, cuts, heavy, held_as=jnp.bfloat16):
    values = spread * jax.random.normal(stream_key, extent, jnp.float32)
    if cuts:
        values = values * block_scale(stream_key, extent, cuts, -0.22, 0.18)
    return jnp.clip(with_spikes(values, jax.random.fold_in(stream_key, 3), *heavy), -limit, limit).astype(held_as)


def setup_inputs(seed: int = 0) -> dict:
    keys = jax.random.split(jax.random.key(seed), 10)
    return {
        "weight": normal_values(keys[0], (ROWS, QKV), 0.5, 3.0, ((1, 8),), jnp.float32),
        "grad_parts": bell_draw_with(keys[1], (N_DP, ROWS, QKV), 1.0, 6.0, ((0, 16), (2, 8)), (0, 1, 16, 2.0), jnp.float32),
        "m_codes": plant(jax.random.randint(keys[2], (NBLK, BLOCK), 0, CODES), jax.random.fold_in(keys[2], 1), 0, CODES - 1).astype(jnp.int32),
        "v_codes": plant(jax.random.randint(keys[3], (NBLK, BLOCK), 0, CODES), jax.random.fold_in(keys[3], 1), 0, CODES - 1).astype(jnp.int32),
        "m_absmax": jnp.clip(jnp.exp(math.log(1.0) - 2.3025851 * jax.random.uniform(keys[4], (NBLK,), jnp.float32) ** block_scale(keys[4], (NBLK,), ((0, 128),), -0.2, 0.2)), 0.1, 1.0),
        "v_absmax": jnp.clip(jnp.exp(math.log(0.01) - 2.30258502 * jax.random.uniform(keys[5], (NBLK,), jnp.float32) ** block_scale(keys[5], (NBLK,), ((0, 128),), -0.2, 0.2)), 0.001, 0.01),
        "code_m": jnp.clip(jax.random.uniform(keys[6], (CODES,), jnp.float32, -1.0, 1.0), -1.0, 1.0),
        "code_v": jnp.clip(jax.random.uniform(keys[7], (CODES,), jnp.float32, 0.05, 1.0), 0.05, 1.0),
        "step": jax.random.randint(keys[8], (1,), 1, 65).astype(jnp.int32),
    }


beta_one = 0.9
beta_two = 0.999
adam_eps = 1e-08
learn_rate = 0.02
decay_rate = 0.1
scale_eps = 1e-06

def reference(weight, grad_parts, m_codes, v_codes, m_absmax, v_absmax, code_m, code_v, step):
    grad = lax.optimization_barrier(jnp.sum(grad_parts, axis=0)).reshape(NBLK, BLOCK)
    m_old = code_m[m_codes] * m_absmax[:, None]
    v_old = code_v[v_codes] * v_absmax[:, None]
    m_new = beta_one * m_old + (1.0 - beta_one) * grad
    v_new = beta_two * v_old + (1.0 - beta_two) * grad * grad
    count = step[0].astype(jnp.float32)
    fix_one = 1.0 - jnp.power(jnp.float32(beta_one), count)
    fix_two = 1.0 - jnp.power(jnp.float32(beta_two), count)
    update = m_new / fix_one / (jnp.sqrt(v_new / fix_two) + adam_eps)
    new_weight = weight - learn_rate * (update.reshape(ROWS, QKV) + decay_rate * weight)
    m_absmax_new = lax.optimization_barrier(jnp.max(jnp.abs(m_new), axis=1))
    v_absmax_new = lax.optimization_barrier(jnp.max(v_new, axis=1))
    m_scaled = (m_new / (m_absmax_new[:, None] + scale_eps)).astype(jnp.bfloat16)
    v_scaled = (v_new / (v_absmax_new[:, None] + scale_eps)).astype(jnp.bfloat16)
    return (new_weight, m_scaled, v_scaled, m_absmax_new, v_absmax_new)
```

```python
import jax
import jax.numpy as jnp
from jax import lax
from jax.sharding import Mesh, PartitionSpec as P

BLOCK = 2048
N_YH, N_Z, N_CORE, N_YL, N_X = 2, 4, 2, 2, 4
AXES = ("yh", "z", "core", "yl", "x")
DP = ("yh", "z", "core")
TENSOR = ("yl", "x")
ROW_OWNERS = ("core", "yl", "x")
PARTS = 2

beta_one = 0.9
beta_two = 0.999
adam_eps = 1e-08
learn_rate = 0.02
decay_rate = 0.1
scale_eps = 1e-06

SWAP = [(0, 1), (1, 0)]
UP = [(i, (i + 1) % N_Z) for i in range(N_Z)]
DOWN = [(i, (i - 1) % N_Z) for i in range(N_Z)]


def lookup(codes, table):
    high = codes // 16
    low = codes - high * 16
    digits = lax.broadcasted_iota(jnp.int32, (16, 1, 1), 0)
    low_hits = (low[None, :, :] == digits).astype(jnp.float32)
    grid = table.reshape(16, 16)
    picked = jnp.einsum("jk,krb->jrb", grid, low_hits, precision=lax.Precision.HIGHEST)
    high_hits = high[None, :, :] == digits
    return jnp.sum(jnp.where(high_hits, picked, jnp.float32(0.0)), axis=0)


def tile(array, yh, z):
    where = (yh * N_Z + z % N_Z) * 128
    return lax.dynamic_slice_in_dim(array, where, 128, axis=1)


def reduce_part(grad_t, part, width, half, c, z, h):
    send = lax.dynamic_slice_in_dim(grad_t, (1 - c) * half + part * width, width, axis=0)
    other = lax.ppermute(send, "core", SWAP)
    own = lax.dynamic_slice_in_dim(grad_t, c * half + part * width, width, axis=0) + other
    up = lax.ppermute(jnp.stack([tile(own, 0, z + 2), tile(own, 1, z + 1)]), "z", UP)
    down = lax.ppermute(jnp.stack([tile(own, 1, z + 2), tile(own, 0, z + 3)]), "z", DOWN)
    up2 = lax.ppermute(tile(own, 0, z + 1) + up[0], "z", UP)
    down2 = lax.ppermute(tile(own, 1, z + 3) + down[0], "z", DOWN)
    low = tile(own, 0, z) + down[1] + up2
    high = tile(own, 1, z) + up[1] + down2
    far = lax.ppermute(jnp.where(h == 0, high, low), "yh", SWAP)
    return jnp.where(h == 0, low, high) + far


def gather_part(mine, h):
    far = lax.ppermute(mine, "yh", SWAP)
    low = jnp.where(h == 0, mine, far)
    high = jnp.where(h == 0, far, mine)
    both = jnp.stack([low, high])
    up = lax.ppermute(both, "z", UP)
    down = lax.ppermute(both, "z", DOWN)
    up2 = lax.ppermute(up[0], "z", UP)
    down2 = lax.ppermute(down[1], "z", DOWN)
    return both, up, down, jnp.stack([up2, down2])


def shards(weight, grad_parts, m_codes, v_codes, m_absmax, v_absmax, code_m, code_v, step):
    rows, columns = weight.shape
    half = columns // N_CORE
    width = half // PARTS
    owners = N_CORE * N_YL * N_X
    c = lax.axis_index("core")
    z = lax.axis_index("z")
    h = lax.axis_index("yh")
    grad_t = grad_parts[0].T
    weight_t = weight.T
    row_tile = rows // (N_YH * N_Z)
    dev_rows = row_tile // owners
    count = step[0].astype(jnp.float32)
    fix_one = 1.0 - jnp.power(jnp.float32(beta_one), count)
    fix_two = 1.0 - jnp.power(jnp.float32(beta_two), count)

    def spread(state):
        wide = state.reshape(dev_rows, N_YL * N_X, N_CORE, PARTS, width)
        return wide.transpose(3, 2, 1, 0, 4).reshape(PARTS, owners, dev_rows, width)

    def collect(parts):
        whole = jnp.stack(parts).reshape(PARTS, N_CORE, N_YL * N_X, dev_rows, width)
        return whole.transpose(3, 2, 1, 0, 4).reshape(-1, BLOCK)

    m_old = spread(lookup(m_codes, code_m) * m_absmax[:, None])
    v_old = spread(lookup(v_codes, code_v) * v_absmax[:, None])

    m_parts, v_parts, pieces = [], [], []
    for part in range(PARTS):
        mine = reduce_part(grad_t, part, width, half, c, z, h)
        sent = mine.T.reshape(owners, dev_rows, width)
        grad = lax.all_to_all(sent, ROW_OWNERS, split_axis=0, concat_axis=0, tiled=True)
        m_new = beta_one * m_old[part] + (1.0 - beta_one) * grad
        v_new = beta_two * v_old[part] + (1.0 - beta_two) * grad * grad
        m_parts.append(m_new)
        v_parts.append(v_new)
        update = m_new / fix_one / (jnp.sqrt(v_new / fix_two) + adam_eps)
        back = lax.all_to_all(update, ROW_OWNERS, split_axis=0, concat_axis=0, tiled=True)
        got = gather_part(back.reshape(row_tile, width).T, h)
        pieces.append([(g, lax.ppermute(g, "core", SWAP)) for g in got])

    halves = []
    for core in range(N_CORE):
        for part in range(PARTS):
            near, up, down, far = [jnp.where(c == core, g, o) for g, o in pieces[part]]
            ring = jnp.stack([near, down, far, up])
            tiles = [lax.dynamic_index_in_dim(ring, (k - z) % N_Z, 0, keepdims=False) for k in range(N_Z)]
            halves.append(jnp.concatenate([t[yh] for yh in range(N_YH) for t in tiles], axis=1))
    mine_t = jnp.concatenate(halves, axis=0)
    new_weight = (weight_t - learn_rate * (mine_t + decay_rate * weight_t)).T

    m_new = collect(m_parts)
    v_new = collect(v_parts)
    m_absmax_new = jnp.max(jnp.abs(m_new), axis=1)
    v_absmax_new = jnp.max(v_new, axis=1)
    m_scaled = (m_new / (m_absmax_new[:, None] + scale_eps)).astype(jnp.bfloat16)
    v_scaled = (v_new / (v_absmax_new[:, None] + scale_eps)).astype(jnp.bfloat16)
    return (new_weight, m_scaled, v_scaled, m_absmax_new, v_absmax_new)


def solution(mesh):
    fine = Mesh(mesh.devices.reshape(N_YH, N_Z, N_CORE, N_YL, N_X), AXES)
    blocks = P(DP + TENSOR)
    in_specs = (P(None, TENSOR), P(DP, None, TENSOR), blocks, blocks, blocks, blocks, P(), P(), P())
    out_specs = (P(None, TENSOR), blocks, blocks, blocks, blocks)
    return jax.shard_map(shards, mesh=fine, in_specs=in_specs, out_specs=out_specs, check_vma=False)
```

```python
import functools

import jax
import jax.numpy as jnp
from jax import lax
from jax.experimental import pallas as pl
from jax.experimental.pallas import tpu as pltpu
from jax.sharding import Mesh, PartitionSpec as P

BLOCK = 2048
LANES = 128
N_YH, N_Z, N_CORE, N_YL, N_X = 2, 4, 2, 2, 4
N_TENSOR = N_YL * N_X
OWNERS = N_CORE * N_TENSOR
AXES = ("yh", "z", "core", "yl", "x")
DP = ("yh", "z", "core")
TENSOR = ("yl", "x")
ROW_OWNERS = ("yh", "core", "yl", "x")
PARTS = 2

beta_one = 0.9
beta_two = 0.999
adam_eps = 1e-08
learn_rate = 0.02
decay_rate = 0.1
scale_eps = 1e-06

SWAP = [(0, 1), (1, 0)]
UP = [(i, (i + 1) % N_Z) for i in range(N_Z)]
DOWN = [(i, (i - 1) % N_Z) for i in range(N_Z)]

ANY = pl.BlockSpec(memory_space=pl.ANY)
SMEM = pl.BlockSpec(memory_space=pltpu.SMEM)
VMEM = pl.BlockSpec(memory_space=pltpu.VMEM)
f32 = jnp.float32


def shape(*dims):
    return jax.ShapeDtypeStruct(dims, f32)


def params():
    return pltpu.CompilerParams(vmem_limit_bytes=40 * 2**20)


def lane_tile(yh, z):
    return pl.ds(pl.multiple_of((yh * N_Z + lax.rem(z, N_Z)) * LANES, LANES), LANES)


def lookup_kernel(m_codes, v_codes, m_scale, v_scale, code_m, code_v, m_out, v_out):
    rows = m_codes.shape[0]
    for codes, scale, table, out in ((m_codes, m_scale, code_m, m_out), (v_codes, v_scale, code_v, v_out)):
        for r in range(0, rows, 8):
            low = jnp.broadcast_to(table[0:1, :], (8, LANES))
            high = jnp.broadcast_to(table[1:2, :], (8, LANES))
            factor = scale[r : r + 8, :]
            for k in range(0, BLOCK, LANES):
                index = codes[r : r + 8, k : k + LANES]
                lane = index & (LANES - 1)
                a = jnp.take_along_axis(low, lane, axis=1)
                b = jnp.take_along_axis(high, lane, axis=1)
                out[r : r + 8, k : k + LANES] = jnp.where(index < LANES, a, b) * factor


def lookup(m_codes, v_codes, m_absmax, v_absmax, code_m, code_v):
    blocks = m_codes.shape[0]
    step = 32
    wide = pl.BlockSpec((step, BLOCK), lambda i: (i, 0))
    thin = pl.BlockSpec((step, 1), lambda i: (i, 0))
    table = pl.BlockSpec((2, LANES), lambda i: (0, 0))
    return pl.pallas_call(
        lookup_kernel,
        grid=(pl.cdiv(blocks, step),),
        in_specs=[wide, wide, thin, thin, table, table],
        out_specs=[wide, wide],
        out_shape=[shape(blocks, BLOCK)] * 2,
        compiler_params=params(),
        name="lookup",
    )(m_codes, v_codes, m_absmax[:, None], v_absmax[:, None], code_m.reshape(2, LANES), code_v.reshape(2, LANES))


def spread_kernel(half, width, m_in, v_in, m_out, v_out):
    for src, dst in ((m_in, m_out), (v_in, v_out)):
        for part in range(PARTS):
            for owner in range(OWNERS):
                c, j = divmod(owner, N_TENSOR)
                at = j * N_CORE * half + c * half + part * width
                dst[part, owner] = src[:, at : at + width]


def collect_kernel(half, width, *refs):
    ins, outs = refs[: 2 * PARTS], refs[2 * PARTS :]
    for which, dst in enumerate(outs):
        for part in range(PARTS):
            for owner in range(OWNERS):
                c, j = divmod(owner, N_TENSOR)
                at = j * N_CORE * half + c * half + part * width
                dst[:, at : at + width] = ins[which * PARTS + part][owner]


def slice_kernel(part, width, side, place, grad, out, sem):
    c = place[0] if side == 0 else 1 - place[0]
    at = pl.multiple_of(c * (width * PARTS) + part * width, 8)
    copy = pltpu.make_async_copy(grad.at[pl.ds(at, width)], out, sem)
    copy.start()
    copy.wait()


def take_slice(place, grad_t, part, width, side):
    return pl.pallas_call(
        functools.partial(slice_kernel, part, width, side),
        in_specs=[SMEM, ANY],
        out_specs=VMEM,
        out_shape=shape(width, grad_t.shape[1]),
        scratch_shapes=[pltpu.SemaphoreType.DMA],
        compiler_params=params(),
        name="take_slice",
    )(place, grad_t)


def pack_kernel(place, own, other, up, down, keep):
    z = place[1]
    picks = (
        (up, 0, 0, z + 2),
        (up, 1, 1, z + 1),
        (down, 0, 1, z + 2),
        (down, 1, 0, z + 3),
        (keep, 0, 0, z + 1),
        (keep, 1, 1, z + 3),
        (keep, 2, 0, z),
        (keep, 3, 1, z),
    )
    for dst, slot, yh, to in picks:
        lanes = lane_tile(yh, to)
        dst[slot] = own[:, lanes] + other[:, lanes]


def relay_kernel(keep, up, down, up2, down2, rest):
    up2[...] = keep[0] + up[0]
    down2[...] = keep[1] + down[0]
    rest[0] = keep[2] + down[1]
    rest[1] = keep[3] + up[1]


def turn_kernel(width, rest, up2, down2, out, held):
    for yh, last in enumerate((up2, down2)):
        held[0:width, :] = rest[yh] + last[...]
        out[yh * LANES : (yh + 1) * LANES, :] = held[...].T[:, :width]


def reduce_part(place, grad_t, part, width):
    rows = grad_t.shape[1]
    send = take_slice(place, grad_t, part, width, 1)
    other = lax.ppermute(send, "core", SWAP)
    own = take_slice(place, grad_t, part, width, 0)
    up, down, keep = pl.pallas_call(
        pack_kernel,
        in_specs=[SMEM, VMEM, VMEM],
        out_specs=[VMEM] * 3,
        out_shape=[shape(2, width, LANES), shape(2, width, LANES), shape(4, width, LANES)],
        compiler_params=params(),
        name="pack",
    )(place, own, other)
    up = lax.ppermute(up, "z", UP)
    down = lax.ppermute(down, "z", DOWN)
    up2, down2, rest = pl.pallas_call(
        relay_kernel,
        in_specs=[VMEM] * 3,
        out_specs=[VMEM] * 3,
        out_shape=[shape(width, LANES), shape(width, LANES), shape(2, width, LANES)],
        compiler_params=params(),
        name="relay",
    )(keep, up, down)
    up2 = lax.ppermute(up2, "z", UP)
    down2 = lax.ppermute(down2, "z", DOWN)
    turned = pl.pallas_call(
        functools.partial(turn_kernel, width),
        in_specs=[VMEM] * 3,
        out_specs=VMEM,
        out_shape=shape(N_YH * LANES, width),
        scratch_shapes=[pltpu.VMEM((pl.cdiv(width, LANES) * LANES, LANES), f32)],
        compiler_params=params(),
        name="turn",
    )(rest, up2, down2)
    sent = turned.reshape(N_YH * OWNERS, -1, width)
    return lax.all_to_all(sent, ROW_OWNERS, split_axis=0, concat_axis=0, tiled=True)


def adam_kernel(fixes, grads, m_old, v_old, m_out, v_out, update):
    grad = grads[:OWNERS] + grads[OWNERS:]
    m_new = beta_one * m_old[...] + (1.0 - beta_one) * grad
    v_new = beta_two * v_old[...] + (1.0 - beta_two) * grad * grad
    m_out[...] = m_new
    v_out[...] = v_new
    step = m_new / fixes[0] / (jnp.sqrt(v_new / fixes[1]) + adam_eps)
    update[:OWNERS] = step
    update[OWNERS:] = step


def adam(fixes, grads, m_old, v_old):
    return pl.pallas_call(
        adam_kernel,
        in_specs=[SMEM, VMEM, VMEM, VMEM],
        out_specs=[VMEM] * 3,
        out_shape=[shape(*m_old.shape), shape(*m_old.shape), shape(*grads.shape)],
        compiler_params=params(),
        name="adam",
    )(fixes, grads, m_old, v_old)


def unturn_kernel(width, rows, out, held):
    for yh in range(N_YH):
        held[:, 0:width] = rows[yh * LANES : (yh + 1) * LANES, :]
        out[yh] = held[...].T[:width, :]


def gather_part(update, width):
    back = lax.all_to_all(update, ROW_OWNERS, split_axis=0, concat_axis=0, tiled=True)
    near = pl.pallas_call(
        functools.partial(unturn_kernel, width),
        in_specs=[VMEM],
        out_specs=VMEM,
        out_shape=shape(N_YH, width, LANES),
        scratch_shapes=[pltpu.VMEM((LANES, pl.cdiv(width, LANES) * LANES), f32)],
        compiler_params=params(),
        name="unturn",
    )(back.reshape(N_YH * LANES, width))
    up = lax.ppermute(near, "z", UP)
    down = lax.ppermute(near, "z", DOWN)
    up2 = lax.ppermute(up[0], "z", UP)
    down2 = lax.ppermute(down[1], "z", DOWN)
    own = [near, up, down, up2, down2]
    return own + [lax.ppermute(g, "core", SWAP) for g in own]


def weight_kernel(part, width, place, weight, *refs):
    pieces, (out, held, in_sem, out_sem) = refs[:10], refs[-4:]
    c, z = place[0], place[1]

    def rows(side):
        core = c if side == 0 else 1 - c
        return pl.ds(pl.multiple_of(core * (width * PARTS) + part * width, 8), width)

    loads = [pltpu.make_async_copy(weight.at[rows(s)], held.at[s], in_sem.at[s]) for s in range(2)]
    stores = [pltpu.make_async_copy(held.at[s], out.at[rows(s)], out_sem.at[s]) for s in range(2)]
    for load in loads:
        load.start()
    for side in range(2):
        near, up, down, up2, down2 = pieces[5 * side : 5 * side + 5]
        loads[side].wait()
        for yh in range(N_YH):
            far = (up2, down2)[yh]
            for piece, at in ((near.at[yh], z), (up.at[yh], z + 3), (down.at[yh], z + 1), (far, z + 2)):
                lanes = lane_tile(yh, at)
                old = held[side, :, lanes]
                held[side, :, lanes] = old - learn_rate * (piece[...] + decay_rate * old)
        stores[side].start()
    for store in stores:
        store.wait()


def write_weight(place, weight_t, pieces, so_far, part, width):
    done = [] if so_far is None else [so_far]
    return pl.pallas_call(
        functools.partial(weight_kernel, part, width),
        in_specs=[SMEM, ANY] + [VMEM] * 10 + [ANY] * len(done),
        out_specs=ANY,
        out_shape=shape(*weight_t.shape),
        input_output_aliases={12: 0} if done else {},
        scratch_shapes=[
            pltpu.VMEM((2, width, weight_t.shape[1]), f32),
            pltpu.SemaphoreType.DMA((2,)),
            pltpu.SemaphoreType.DMA((2,)),
        ],
        compiler_params=params(),
        name="write_weight",
    )(place, weight_t, *pieces, *done)


def shards(weight, grad_parts, m_codes, v_codes, m_absmax, v_absmax, code_m, code_v, step):
    columns = weight.shape[1]
    half = columns // N_CORE
    width = half // PARTS
    dev_rows = LANES // OWNERS
    place = jnp.stack([lax.axis_index("core"), lax.axis_index("z")]).astype(jnp.int32)
    grad_t = grad_parts[0].T
    weight_t = weight.T
    count = step[0].astype(f32)
    fix_one = 1.0 - jnp.power(f32(beta_one), count)
    fix_two = 1.0 - jnp.power(f32(beta_two), count)
    fixes = jnp.stack([fix_one, fix_two])

    m_old, v_old = lookup(m_codes, v_codes, m_absmax, v_absmax, code_m, code_v)
    flat = (dev_rows, columns * N_TENSOR)
    m_old, v_old = pl.pallas_call(
        functools.partial(spread_kernel, half, width),
        in_specs=[VMEM] * 2,
        out_specs=[VMEM] * 2,
        out_shape=[shape(PARTS, OWNERS, dev_rows, width)] * 2,
        compiler_params=params(),
        name="spread",
    )(m_old.reshape(flat), v_old.reshape(flat))

    m_parts, v_parts, gathered = [], [], []
    for part in range(PARTS):
        grads = reduce_part(place, grad_t, part, width)
        m_new, v_new, update = adam(fixes, grads, m_old[part], v_old[part])
        m_parts.append(m_new)
        v_parts.append(v_new)
        gathered.append(gather_part(update, width))

    new_weight = None
    for part in range(PARTS):
        new_weight = write_weight(place, weight_t, gathered[part], new_weight, part, width)

    m_new, v_new = pl.pallas_call(
        functools.partial(collect_kernel, half, width),
        in_specs=[VMEM] * (2 * PARTS),
        out_specs=[VMEM] * 2,
        out_shape=[shape(*flat)] * 2,
        compiler_params=params(),
        name="collect",
    )(*m_parts, *v_parts)
    m_new = m_new.reshape(-1, BLOCK)
    v_new = v_new.reshape(-1, BLOCK)
    m_absmax_new = jnp.max(jnp.abs(m_new), axis=1)
    v_absmax_new = jnp.max(v_new, axis=1)
    m_scaled = (m_new / (m_absmax_new[:, None] + scale_eps)).astype(jnp.bfloat16)
    v_scaled = (v_new / (v_absmax_new[:, None] + scale_eps)).astype(jnp.bfloat16)
    return (new_weight.T, m_scaled, v_scaled, m_absmax_new, v_absmax_new)


def solution(mesh):
    fine = Mesh(mesh.devices.reshape(N_YH, N_Z, N_CORE, N_YL, N_X), AXES)
    blocks = P(DP + TENSOR)
    in_specs = (P(None, TENSOR), P(DP, None, TENSOR), blocks, blocks, blocks, blocks, P(), P(), P())
    out_specs = (P(None, TENSOR), blocks, blocks, blocks, blocks)
    return jax.shard_map(shards, mesh=fine, in_specs=in_specs, out_specs=out_specs, check_vma=False)
```

```python
import functools

import jax
import jax.numpy as jnp
from jax import lax
from jax.experimental import pallas as pl
from jax.experimental.pallas import tpu as pltpu
from jax.sharding import Mesh, PartitionSpec as P

BLOCK = 2048
LANES = 128
N_YH, N_Z, N_CORE, N_YL, N_X = 2, 4, 2, 2, 4
N_TENSOR = N_YL * N_X
OWNERS = N_CORE * N_TENSOR
AXES = ("yh", "z", "core", "yl", "x")
DP = ("yh", "z", "core")
TENSOR = ("yl", "x")
ROW_OWNERS = ("yh", "core", "yl", "x")
PARTS = 2

beta_one = 0.9
beta_two = 0.999
adam_eps = 1e-08
learn_rate = 0.02
decay_rate = 0.1
scale_eps = 1e-06

SWAP = [(0, 1), (1, 0)]
UP = [(i, (i + 1) % N_Z) for i in range(N_Z)]
DOWN = [(i, (i - 1) % N_Z) for i in range(N_Z)]

ANY = pl.BlockSpec(memory_space=pl.ANY)
SMEM = pl.BlockSpec(memory_space=pltpu.SMEM)
VMEM = pl.BlockSpec(memory_space=pltpu.VMEM)
f32 = jnp.float32
COST = pl.CostEstimate(flops=1, bytes_accessed=1024, transcendentals=0)


def shape(*dims):
    return jax.ShapeDtypeStruct(dims, f32)


def params():
    return pltpu.CompilerParams(vmem_limit_bytes=10 * 2**20)


def lane_tile(yh, z):
    return pl.ds(pl.multiple_of((yh * N_Z + lax.rem(z, N_Z)) * LANES, LANES), LANES)


STEP = 248


def each(count, body):
    @pl.loop(0, count // STEP)
    def _(i):
        for k in range(0, STEP, 8):
            body(pl.multiple_of(i * STEP + k, 8))


def segments(rows, row):
    for r in range(rows):
        at = r * row
        while at < (r + 1) * row:
            end = min((r + 1) * row, (at // BLOCK + 1) * BLOCK)
            b = at // BLOCK
            yield r, slice(at - r * row, end - r * row), b, slice(at - b * BLOCK, end - b * BLOCK)
            at = end


def owned(half, owner):
    c, j = divmod(owner, N_TENSOR)
    at = j * N_CORE * half + c * half
    return slice(at, at + half)


def old_state_kernel(half, m_codes, v_codes, m_scale, v_scale, code_m, code_v, m_out, v_out, held, flat):
    outs = (m_out, v_out)
    blocks = m_codes.shape[0]
    for which, (codes, scale, table) in enumerate(((m_codes, m_scale, code_m), (v_codes, v_scale, code_v))):
        low = jnp.broadcast_to(table[0:1, :], (8, LANES))
        high = jnp.broadcast_to(table[1:2, :], (8, LANES))
        for r in range(0, blocks, 8):
            rows = slice(min(r, blocks - 8), min(r, blocks - 8) + 8)
            for k in range(0, BLOCK, LANES):
                index = codes[rows, k : k + LANES]
                lane = index & (LANES - 1)
                a = jnp.take_along_axis(low, lane, axis=1)
                b = jnp.take_along_axis(high, lane, axis=1)
                held[rows, k : k + LANES] = jnp.where(index < LANES, a, b)
        for r, columns, b, inside in segments(*flat.shape):
            flat[r : r + 1, columns] = held[b : b + 1, inside] * scale[b]
        for owner in range(OWNERS):
            outs[which][owner] = flat[:, owned(half, owner)]


def old_state(m_codes, v_codes, m_absmax, v_absmax, code_m, code_v, half):
    rows = LANES // OWNERS
    return pl.pallas_call(
        functools.partial(old_state_kernel, half),
        in_specs=[VMEM, VMEM, SMEM, SMEM, VMEM, VMEM],
        out_specs=[VMEM] * 2,
        out_shape=[shape(OWNERS, rows, half)] * 2,
        scratch_shapes=[pltpu.VMEM(m_codes.shape, f32), pltpu.VMEM((rows, N_CORE * half * N_TENSOR), f32)],
        compiler_params=params(),
        cost_estimate=COST,
        name="old_state",
    )(m_codes, v_codes, m_absmax, v_absmax, code_m.reshape(2, LANES), code_v.reshape(2, LANES))


def new_state_kernel(half, m_in, v_in, *refs):
    outs, (held, flat) = refs[:4], refs[4:]
    blocks = outs[0].shape[0]
    for which, values in enumerate((m_in, v_in)):
        for owner in range(OWNERS):
            flat[:, owned(half, owner)] = values[owner]
        for r, columns, b, inside in segments(*flat.shape):
            held[b : b + 1, inside] = flat[r : r + 1, columns]
        value = held[...]
        largest = jnp.max(jnp.abs(value) if which == 0 else value, axis=1, keepdims=True)
        outs[which][...] = (value / (largest + scale_eps)).astype(jnp.bfloat16)[:blocks]
        outs[2 + which][...] = jnp.broadcast_to(largest, (held.shape[0], LANES)).T[0:1, :blocks]


def new_state(m_new, v_new, blocks, half):
    rows = LANES // OWNERS
    scaled = jax.ShapeDtypeStruct((blocks, BLOCK), jnp.bfloat16)
    m_scaled, v_scaled, m_absmax, v_absmax = pl.pallas_call(
        functools.partial(new_state_kernel, half),
        in_specs=[VMEM] * 2,
        out_specs=[VMEM] * 4,
        out_shape=[scaled, scaled, shape(1, blocks), shape(1, blocks)],
        scratch_shapes=[
            pltpu.VMEM((pl.cdiv(blocks, 8) * 8, BLOCK), f32),
            pltpu.VMEM((rows, N_CORE * half * N_TENSOR), f32),
        ],
        compiler_params=params(),
        cost_estimate=COST,
        name="new_state",
    )(m_new, v_new)
    return m_scaled, v_scaled, m_absmax[0], v_absmax[0]


def rows_of(core, part, width):
    return pl.ds(pl.multiple_of(core * (width * PARTS) + part * width, 8), width)


def in_hbm(array):
    return pltpu.with_memory_space_constraint(array, pltpu.HBM)


def take_kernel(part, width, place, source, send, sem):
    copy = pltpu.make_async_copy(source.at[rows_of(1 - place[0], part, width)], send, sem)
    copy.start()
    copy.wait()


def take(place, source, part, width, spec):
    return pl.pallas_call(
        functools.partial(take_kernel, part, width),
        in_specs=[SMEM, spec],
        out_specs=VMEM,
        out_shape=shape(width, source.shape[1]),
        scratch_shapes=[pltpu.SemaphoreType.DMA],
        compiler_params=params(),
        cost_estimate=COST,
        name="take_part",
    )(place, source)


def pack_kernel(part, width, place, grad, other, up, down, keep):
    c, z = place[0], place[1]
    base = c * (width * PARTS) + part * width
    spots = (
        (up, 0, 0, 2),
        (down, 0, 1, 2),
        (up, 1, 1, 1),
        (down, 1, 0, 3),
        (keep, 0, 0, 1),
        (keep, 1, 1, 3),
        (keep, 2, 0, 0),
        (keep, 3, 1, 0),
    )

    def body(r):
        own = pl.ds(pl.multiple_of(base + r, 8), 8)
        rows = pl.ds(r, 8)
        for out, slot, yh, to in spots:
            lanes = lane_tile(yh, z + to)
            out[slot, rows, :] = grad[own, lanes] + other[rows, lanes]

    each(width, body)


def pack(place, grad_t, other, part, width):
    outs = [shape(n, width, LANES) for n in (2, 2, 4)]
    return pl.pallas_call(
        functools.partial(pack_kernel, part, width),
        in_specs=[SMEM, VMEM, VMEM],
        out_specs=[VMEM] * 3,
        out_shape=outs,
        compiler_params=params(),
        cost_estimate=COST,
        name="pack",
    )(place, grad_t, other)


def relay_kernel(keep, up, down, up2, down2, rest):
    def body(r):
        rows = pl.ds(r, 8)
        up2[rows, :] = keep[0, rows, :] + up[0, rows, :]
        down2[rows, :] = keep[1, rows, :] + down[0, rows, :]
        rest[0, rows, :] = keep[2, rows, :] + down[1, rows, :]
        rest[1, rows, :] = keep[3, rows, :] + up[1, rows, :]

    each(keep.shape[1], body)


def relay(keep, up, down):
    tile = keep.shape[1:]
    return pl.pallas_call(
        relay_kernel,
        in_specs=[VMEM] * 3,
        out_specs=[VMEM] * 3,
        out_shape=[shape(*tile), shape(*tile), shape(N_YH, *tile)],
        compiler_params=params(),
        cost_estimate=COST,
        name="relay",
    )(keep, up, down)


def ring(up, down):
    return lax.ppermute(up, "z", UP), lax.ppermute(down, "z", DOWN)


def turn_kernel(width, *refs):
    parts, (out, held) = refs[:-2], refs[-2:]
    for yh in range(N_YH):
        for part in range(PARTS):
            rest, arrived = parts[3 * part], parts[3 * part + 1 + yh]
            held[part * width : (part + 1) * width, :] = rest[yh] + arrived[...]
        rows = held[...].T[:, : PARTS * width]
        out[yh * OWNERS : (yh + 1) * OWNERS] = rows.reshape(OWNERS, -1, PARTS * width)


def turn(sums, width):
    return pl.pallas_call(
        functools.partial(turn_kernel, width),
        in_specs=[VMEM] * len(sums),
        out_specs=VMEM,
        out_shape=shape(N_YH * OWNERS, LANES // OWNERS, PARTS * width),
        scratch_shapes=[pltpu.VMEM((pl.cdiv(PARTS * width, LANES) * LANES, LANES), f32)],
        compiler_params=params(),
        cost_estimate=COST,
        name="turn",
    )(*sums)


def exchange(array):
    return lax.all_to_all(array, ROW_OWNERS, split_axis=0, concat_axis=0, tiled=True)


def adam_kernel(fixes, grads, m_old, v_old, m_out, v_out, update):
    def body(owner):
        grad = grads[owner] + grads[OWNERS + owner]
        m_new = beta_one * m_old[owner] + (1.0 - beta_one) * grad
        v_new = beta_two * v_old[owner] + (1.0 - beta_two) * grad * grad
        m_out[owner] = m_new
        v_out[owner] = v_new
        value = m_new / fixes[0] / (jnp.sqrt(v_new / fixes[1]) + adam_eps)
        update[owner] = value
        update[OWNERS + owner] = value

    pl.loop(0, OWNERS)(body)


def adam(fixes, grads, m_old, v_old):
    return pl.pallas_call(
        adam_kernel,
        in_specs=[SMEM] + [VMEM] * 3,
        out_specs=[VMEM] * 3,
        out_shape=[shape(*m_old.shape), shape(*m_old.shape), shape(*grads.shape)],
        compiler_params=params(),
        cost_estimate=COST,
        name="adam",
    )(fixes, grads, m_old, v_old)


def unturn_kernel(width, rows, *refs):
    outs, near, held = refs[:PARTS], refs[PARTS], refs[PARTS + 1]
    for yh in range(N_YH):
        held[:, 0 : PARTS * width] = rows[yh * OWNERS : (yh + 1) * OWNERS].reshape(LANES, PARTS * width)
        turned = held[...].T
        for part, out in enumerate(outs):
            value = turned[part * width : (part + 1) * width, :]
            out[yh] = value
            near[N_YH * part + yh] = value


def unturn(back, width):
    pair = shape(N_YH, width, LANES)
    return pl.pallas_call(
        functools.partial(unturn_kernel, width),
        in_specs=[VMEM],
        out_specs=[VMEM] * (PARTS + 1),
        out_shape=[pair] * PARTS + [shape(PARTS * N_YH, width, LANES)],
        scratch_shapes=[pltpu.VMEM((LANES, pl.cdiv(PARTS * width, LANES) * LANES), f32)],
        compiler_params=params(),
        cost_estimate=COST,
        name="unturn",
    )(back)


def relayed_kernel(up, down, up_out, down_out):
    up_out[...] = up[0]
    down_out[...] = down[1]


def relayed(up, down):
    return pl.pallas_call(
        relayed_kernel,
        in_specs=[VMEM] * 2,
        out_specs=[VMEM] * 2,
        out_shape=[shape(*up.shape[1:])] * 2,
        compiler_params=params(),
        cost_estimate=COST,
        name="relayed",
    )(up, down)


def gathered_kernel(*refs):
    pieces, out = refs[:-1], refs[-1]
    at = 0
    for piece in pieces:
        if len(piece.shape) == 2:
            out[at] = piece[...]
            at += 1
        else:
            out[at : at + piece.shape[0]] = piece[...]
            at += piece.shape[0]


def gathered(*pieces):
    count = sum(p.shape[0] if p.ndim == 3 else 1 for p in pieces)
    return pl.pallas_call(
        gathered_kernel,
        in_specs=[VMEM] * len(pieces),
        out_specs=VMEM,
        out_shape=shape(count, *pieces[0].shape[-2:]),
        compiler_params=params(),
        cost_estimate=COST,
        name="gathered",
    )(*pieces)


def swapped(pieces):
    return list(pieces) + [lax.ppermute(p, "core", SWAP) for p in pieces]


def places_of(width, places, place):
    c, z = place[0], place[1]
    work = []
    for side in range(2):
        for k, spots in enumerate(places):
            for slot, (part, yh, to) in enumerate(spots):
                rows = rows_of(c if side == 0 else 1 - c, part, width)
                work.append((side * len(places) + k, slot, rows, lane_tile(yh, z + to)))
    return work


def weight_kernel(width, places, place, weight, *refs):
    count = 2 * len(places)
    pieces, (out, held, sem) = refs[:count], refs[-3:]
    stores = []
    for k, (piece, slot, spot, lanes) in enumerate(places_of(width, places, place)):

        def body(r):
            rows = pl.ds(r, 8)
            old = weight[pl.ds(pl.multiple_of(spot.start + r, 8), 8), lanes]
            if len(pieces[piece].shape) == 3:
                update = pieces[piece][slot, rows, :]
            else:
                update = pieces[piece][rows, :]
            held[k, rows, :] = old - learn_rate * (update + decay_rate * old)

        each(width, body)
        stores.append(pltpu.make_async_copy(held.at[k], out.at[spot, lanes], sem.at[k]))
        stores[k].start()
    for store in stores:
        store.wait()


def hold_kernel(source, out, sem):
    copy = pltpu.make_async_copy(source, out, sem)
    copy.start()
    copy.wait()


def hold(array):
    return pl.pallas_call(
        hold_kernel,
        in_specs=[pl.BlockSpec(memory_space=pltpu.HBM)],
        out_specs=VMEM,
        out_shape=shape(*array.shape),
        scratch_shapes=[pltpu.SemaphoreType.DMA],
        compiler_params=params(),
        cost_estimate=COST,
        name="hold",
    )(in_hbm(array))


NEAR = (((0, 0, 0), (0, 1, 0), (1, 0, 0), (1, 1, 0)),)
SIDES = (((0, 0, 3), (0, 1, 3), (0, 0, 1), (0, 1, 1), (1, 0, 3), (1, 1, 3), (1, 0, 1), (1, 1, 1), (0, 0, 2), (0, 1, 2)),)
LAST = (((1, 0, 2), (1, 1, 2)),)


def write_weight(place, held, pieces, places, so_far, width):
    done = [] if so_far is None else [so_far]
    stores = 2 * sum(len(spots) for spots in places)
    hbm = pl.BlockSpec(memory_space=pltpu.HBM)
    return pl.pallas_call(
        functools.partial(weight_kernel, width, places),
        in_specs=[SMEM, VMEM] + [VMEM] * len(pieces) + [hbm] * len(done),
        out_specs=hbm,
        out_shape=shape(*held.shape),
        input_output_aliases={2 + len(pieces): 0} if done else {},
        scratch_shapes=[pltpu.VMEM((stores, width, LANES), f32), pltpu.SemaphoreType.DMA((stores,))],
        compiler_params=params(),
        cost_estimate=COST,
        name="write_weight",
    )(place, held, *pieces, *done)


def after(value, *others):
    return lax.optimization_barrier((value, *others))[0]


def shards(weight, grad_parts, m_codes, v_codes, m_absmax, v_absmax, code_m, code_v, step):
    columns = weight.shape[1]
    half = columns // N_CORE
    width = half // PARTS
    place = jnp.stack([lax.axis_index("core"), lax.axis_index("z")]).astype(jnp.int32)
    grad_t = grad_parts[0].T
    weight_t = weight.T

    send_0 = take(place, in_hbm(grad_t), 0, width, pl.BlockSpec(memory_space=pltpu.HBM))
    other_0 = lax.ppermute(send_0, "core", SWAP)
    send_1 = take(after(place, send_0), grad_t, 1, width, VMEM)
    other_1 = lax.ppermute(after(send_1, other_0), "core", SWAP)

    up, down, keep_0 = pack(place, grad_t, other_0, 0, width)
    other_1 = after(other_1, keep_0)
    up_0, down_0 = ring(up, down)
    up, down, keep_1 = pack(place, grad_t, other_1, 1, width)
    up_1, down_1 = ring(up, down)
    up2, down2, rest_0 = relay(keep_0, up_0, down_0)
    keep_1 = after(keep_1, rest_0)
    sums_0 = (rest_0, *ring(up2, down2))
    up2, down2, rest_1 = relay(keep_1, up_1, down_1)
    sums_1 = (rest_1, *ring(up2, down2))

    count = step[0].astype(f32)
    fix_one = 1.0 - jnp.power(f32(beta_one), count)
    fix_two = 1.0 - jnp.power(f32(beta_two), count)
    fixes = jnp.stack([fix_one, fix_two])
    olds = old_state(after(m_codes, rest_1), v_codes, m_absmax, v_absmax, code_m, code_v, half)
    held = hold(after(weight_t, olds[0]))
    *sums, held = lax.optimization_barrier((*sums_0, *sums_1, held, *olds, fixes))[:7]

    grads = exchange(turn(sums, width))
    m_new, v_new, update = adam(fixes, grads, *olds)
    pair_0, pair_1, near = unturn(exchange(update), width)

    up_0, down_0 = ring(pair_0, pair_0)
    up_1, down_1 = ring(pair_1, pair_1)
    new_weight = write_weight(place, held, swapped((near,)), NEAR, None, width)
    state = new_state(m_new, v_new, m_codes.shape[0], half)
    up_0, down_0, new_weight, *state = lax.optimization_barrier((up_0, down_0, new_weight, *state))
    up2, down2 = relayed(up_0, down_0)
    up_1, down_1 = lax.optimization_barrier((up_1, down_1, up2))[:2]
    up2_0, down2_0 = ring(up2, down2)
    up2, down2 = relayed(up_1, down_1)
    sides = gathered(up_0, down_0, up_1, after(down_1, up2), up2_0, down2_0)
    up2, down2 = ring(up2, down2)
    new_weight = write_weight(place, held, swapped((sides,)), SIDES, new_weight, width)
    far = lax.optimization_barrier((up2, down2, new_weight))
    new_weight = write_weight(place, held, swapped((gathered(*far[:2]),)), LAST, far[2], width)
    return (new_weight.T, *state)


def solution(mesh):
    fine = Mesh(mesh.devices.reshape(N_YH, N_Z, N_CORE, N_YL, N_X), AXES)
    blocks = P(DP + TENSOR)
    in_specs = (P(None, TENSOR), P(DP, None, TENSOR), blocks, blocks, blocks, blocks, P(), P(), P())
    out_specs = (P(None, TENSOR), blocks, blocks, blocks, blocks)
    return jax.shard_map(shards, mesh=fine, in_specs=in_specs, out_specs=out_specs, check_vma=False)
```

```python
import functools

import jax
import jax.numpy as jnp
from jax import lax
from jax.experimental import pallas as pl
from jax.experimental.pallas import tpu as pltpu
from jax.sharding import Mesh, PartitionSpec as P

BLOCK = 2048
LANES = 128
N_YH, N_Z, N_CORE, N_YL, N_X = 2, 4, 2, 2, 4
N_TENSOR = N_YL * N_X
OWNERS = N_CORE * N_TENSOR
AXES = ("yh", "z", "core", "yl", "x")
DP = ("yh", "z", "core")
TENSOR = ("yl", "x")
ROW_OWNERS = ("yh", "core", "yl", "x")
WIDTH = 400
BACK = 496
FIRST = 192
HALF = FIRST // 2
PLAIN = 2 * WIDTH
SENT = PLAIN + HALF

beta_one = 0.9
beta_two = 0.999
adam_eps = 1e-08
learn_rate = 0.02
decay_rate = 0.1
scale_eps = 1e-06

SWAP = [(0, 1), (1, 0)]
UP = [(i, (i + 1) % N_Z) for i in range(N_Z)]
DOWN = [(i, (i - 1) % N_Z) for i in range(N_Z)]
ACROSS = [(i, (i + 2) % N_Z) for i in range(N_Z)]

ANY = pl.BlockSpec(memory_space=pl.ANY)
SMEM = pl.BlockSpec(memory_space=pltpu.SMEM)
VMEM = pl.BlockSpec(memory_space=pltpu.VMEM)
f32 = jnp.float32
COST = pl.CostEstimate(flops=1, bytes_accessed=1024, transcendentals=0)


def shape(*dims):
    return jax.ShapeDtypeStruct(dims, f32)


def params():
    return pltpu.CompilerParams(vmem_limit_bytes=10 * 2**20)


def lane_tile(yh, z):
    return pl.ds(pl.multiple_of((yh * N_Z + lax.rem(z, N_Z)) * LANES, LANES), LANES)


def each(count, body):
    for r in range(0, count, 8):
        body(slice(r, r + 8))


def segments(rows, row):
    for r in range(rows):
        at = r * row
        while at < (r + 1) * row:
            end = min((r + 1) * row, (at // BLOCK + 1) * BLOCK)
            b = at // BLOCK
            yield r, slice(at - r * row, end - r * row), b, slice(at - b * BLOCK, end - b * BLOCK)
            at = end


def owned(half, owner):
    c, j = divmod(owner, N_TENSOR)
    at = j * N_CORE * half + c * half
    return slice(at, at + half)


def old_state_kernel(half, m_codes, v_codes, m_scale, v_scale, code_m, code_v, m_out, v_out, held, flat):
    outs = (m_out, v_out)
    blocks = m_codes.shape[0]
    for which, (codes, scale, table) in enumerate(((m_codes, m_scale, code_m), (v_codes, v_scale, code_v))):
        low = jnp.broadcast_to(table[0:1, :], (8, LANES))
        high = jnp.broadcast_to(table[1:2, :], (8, LANES))
        for r in range(0, blocks, 8):
            rows = slice(min(r, blocks - 8), min(r, blocks - 8) + 8)
            for k in range(0, BLOCK, LANES):
                index = codes[rows, k : k + LANES]
                lane = index & (LANES - 1)
                a = jnp.take_along_axis(low, lane, axis=1)
                b = jnp.take_along_axis(high, lane, axis=1)
                held[rows, k : k + LANES] = jnp.where(index < LANES, a, b)
        for r, columns, b, inside in segments(*flat.shape):
            flat[r : r + 1, columns] = held[b : b + 1, inside] * scale[b]
        for owner in range(OWNERS):
            outs[which][owner] = flat[:, owned(half, owner)]


def old_state(m_codes, v_codes, m_absmax, v_absmax, code_m, code_v, half):
    rows = LANES // OWNERS
    return pl.pallas_call(
        functools.partial(old_state_kernel, half),
        in_specs=[VMEM, VMEM, SMEM, SMEM, VMEM, VMEM],
        out_specs=[VMEM] * 2,
        out_shape=[shape(OWNERS, rows, half)] * 2,
        scratch_shapes=[pltpu.VMEM(m_codes.shape, f32), pltpu.VMEM((rows, N_CORE * half * N_TENSOR), f32)],
        compiler_params=params(),
        cost_estimate=COST,
        name="old_state",
    )(m_codes, v_codes, m_absmax, v_absmax, code_m.reshape(2, LANES), code_v.reshape(2, LANES))


def new_state_kernel(half, m_in, v_in, *refs):
    outs, (held, flat) = refs[:4], refs[4:]
    blocks = outs[0].shape[0]
    for which, values in enumerate((m_in, v_in)):
        for owner in range(OWNERS):
            flat[:, owned(half, owner)] = values[owner]
        for r, columns, b, inside in segments(*flat.shape):
            held[b : b + 1, inside] = flat[r : r + 1, columns]
        value = held[...]
        largest = jnp.max(jnp.abs(value) if which == 0 else value, axis=1, keepdims=True)
        outs[which][...] = (value / (largest + scale_eps)).astype(jnp.bfloat16)[:blocks]
        outs[2 + which][...] = jnp.broadcast_to(largest, (held.shape[0], LANES)).T[0:1, :blocks]


def new_state(m_new, v_new, blocks, half):
    rows = LANES // OWNERS
    scaled = jax.ShapeDtypeStruct((blocks, BLOCK), jnp.bfloat16)
    m_scaled, v_scaled, m_absmax, v_absmax = pl.pallas_call(
        functools.partial(new_state_kernel, half),
        in_specs=[VMEM] * 2,
        out_specs=[VMEM] * 4,
        out_shape=[scaled, scaled, shape(1, blocks), shape(1, blocks)],
        scratch_shapes=[
            pltpu.VMEM((pl.cdiv(blocks, 8) * 8, BLOCK), f32),
            pltpu.VMEM((rows, N_CORE * half * N_TENSOR), f32),
        ],
        compiler_params=params(),
        cost_estimate=COST,
        name="new_state",
    )(m_new, v_new)
    return m_scaled, v_scaled, m_absmax[0], v_absmax[0]


def in_hbm(array):
    return pltpu.with_memory_space_constraint(array, pltpu.HBM)


def columns_at(core, half, start, width):
    return pl.ds(pl.multiple_of(core * half + start, 8), width)


def take_kernel(half, start, place, source, send, sem):
    rows = columns_at(1 - place[0], half, start, send.shape[0])
    copy = pltpu.make_async_copy(source.at[rows], send, sem)
    copy.start()
    copy.wait()


def take(place, source, start, width, spec):
    return pl.pallas_call(
        functools.partial(take_kernel, source.shape[0] // N_CORE, start),
        in_specs=[SMEM, spec],
        out_specs=VMEM,
        out_shape=shape(width, source.shape[1]),
        scratch_shapes=[pltpu.SemaphoreType.DMA],
        compiler_params=params(),
        cost_estimate=COST,
        name="take_part",
    )(place, source)


def pack_tiles(place, source, base, other, up, down, keep):
    z = place[1]
    rows = other.shape[0]
    for out, slot, yh, to in (
        (up, 0, 0, 2),
        (down, 0, 1, 2),
        (up, 1, 1, 1),
        (down, 1, 0, 3),
        (keep, 0, 0, 1),
        (keep, 1, 1, 3),
        (keep, 2, 0, 0),
        (keep, 3, 1, 0),
    ):
        lanes = lane_tile(yh, z + to)
        one = source.at[pl.ds(pl.multiple_of(base, 8), rows), lanes]
        two = other.at[:, lanes]

        def body(r):
            out[slot, r, :] = one[r, :] + two[r, :]

        each(rows, body)


def pack_kernel(half, start, place, source, other, up, down, keep):
    pack_tiles(place, source, place[0] * half + start, other, up, down, keep)


def packed(width):
    return [shape(n, width, LANES) for n in (2, 2, 4)]


def pack(place, source, other, half, start):
    return pl.pallas_call(
        functools.partial(pack_kernel, half, start),
        in_specs=[SMEM, VMEM, VMEM],
        out_specs=[VMEM] * 3,
        out_shape=packed(other.shape[0]),
        compiler_params=params(),
        cost_estimate=COST,
        name="pack",
    )(place, source, other)


def pack_rest_kernel(half, place, grad, other, up, down, keep, send, mine):
    c, yh = place[0], place[2]
    for out, which in ((send, 1 - yh), (mine, yh)):
        at = which * HALF
        one = grad.at[pl.ds(pl.multiple_of(c * half + PLAIN + at, 8), HALF)]
        two = other.at[pl.ds(pl.multiple_of(WIDTH + at, 8), HALF)]

        def body(r):
            out[r, :] = one[r, :] + two[r, :]

        each(HALF, body)
    pack_tiles(place, grad, c * half + WIDTH, other.at[:WIDTH], up, down, keep)


def pack_rest(place, grad_t, other):
    return pl.pallas_call(
        functools.partial(pack_rest_kernel, grad_t.shape[0] // N_CORE),
        in_specs=[SMEM, VMEM, VMEM],
        out_specs=[VMEM] * 5,
        out_shape=packed(WIDTH) + [shape(HALF, grad_t.shape[1])] * 2,
        compiler_params=params(),
        cost_estimate=COST,
        name="pack_rest",
    )(place, grad_t, other)


def relay_kernel(keep, up, down, up2, down2, rest):
    def body(r):
        up2[r, :] = keep[0, r, :] + up[0, r, :]
        down2[r, :] = keep[1, r, :] + down[0, r, :]
        rest[0, r, :] = keep[2, r, :] + down[1, r, :]
        rest[1, r, :] = keep[3, r, :] + up[1, r, :]

    each(keep.shape[1], body)


def relay(keep, up, down):
    tile = keep.shape[1:]
    return pl.pallas_call(
        relay_kernel,
        in_specs=[VMEM] * 3,
        out_specs=[VMEM] * 3,
        out_shape=[shape(*tile), shape(*tile), shape(N_YH, *tile)],
        compiler_params=params(),
        cost_estimate=COST,
        name="relay",
    )(keep, up, down)


def relay_pack_kernel(place, keep, up, down, mine, arrived, up2, down2, across, rest, own):
    z = place[1]

    def body(r):
        up2[r, :] = keep[0, r, :] + up[0, r, :]
        down2[r, :] = keep[1, r, :] + down[0, r, :]
        rest[0, r, :] = keep[2, r, :] + down[1, r, :]
        rest[1, r, :] = keep[3, r, :] + up[1, r, :]

    each(WIDTH, body)
    for yh in range(N_YH):
        part = pl.ds(WIDTH + yh * HALF, HALF)
        for out, to in ((own.at[yh], 0), (up2.at[part], 1), (across.at[yh], 2), (down2.at[part], 3)):
            lanes = lane_tile(yh, z + to)
            one, two = mine.at[:, lanes], arrived.at[:, lanes]

            def third(r):
                out[r, :] = one[r, :] + two[r, :]

            each(HALF, third)


def relay_pack(place, keep, up, down, mine, arrived):
    sent = shape(WIDTH + N_YH * HALF, LANES)
    third = shape(N_YH, HALF, LANES)
    return pl.pallas_call(
        relay_pack_kernel,
        in_specs=[SMEM] + [VMEM] * 5,
        out_specs=[VMEM] * 5,
        out_shape=[sent, sent, third, shape(N_YH, WIDTH, LANES), third],
        compiler_params=params(),
        cost_estimate=COST,
        name="relay_pack",
    )(place, keep, up, down, mine, arrived)


def ring(up, down):
    return lax.ppermute(up, "z", UP), lax.ppermute(down, "z", DOWN)


def turn_kernel(rest_0, up_0, down_0, own, across, rest_1, up_1, down_1, out, held):
    for yh in range(N_YH):
        low, high = ((up_0, up_1), (down_0, down_1))[yh]
        held[:WIDTH, :] = rest_0[yh] + low[:WIDTH, :]
        held[WIDTH:PLAIN, :] = rest_1[yh] + high[...]
        part = pl.ds(WIDTH + yh * HALF, HALF)
        held[PLAIN:SENT, :] = own[yh] + up_0[part, :] + down_0[part, :] + across[yh]
        out[yh * OWNERS : (yh + 1) * OWNERS] = held[...].T[:, :SENT].reshape(OWNERS, -1, SENT)


def turn(sums):
    return pl.pallas_call(
        turn_kernel,
        in_specs=[VMEM] * len(sums),
        out_specs=VMEM,
        out_shape=shape(N_YH * OWNERS, LANES // OWNERS, SENT),
        scratch_shapes=[pltpu.VMEM((pl.cdiv(SENT, LANES) * LANES, LANES), f32)],
        compiler_params=params(),
        cost_estimate=COST,
        name="turn",
    )(*sums)


def exchange(array):
    return lax.all_to_all(array, ROW_OWNERS, split_axis=0, concat_axis=0, tiled=True)


def adam_kernel(fixes, grads, m_old, v_old, m_out, v_out, update, held):
    for owner in range(OWNERS):
        held[owner, :, :SENT] = grads[owner]
        held[owner, :, :PLAIN] += grads[OWNERS + owner, :, :PLAIN]
        held[owner, :, SENT:] = grads[OWNERS + owner, :, PLAIN:]
        grad = held[owner]
        m_new = beta_one * m_old[owner] + (1.0 - beta_one) * grad
        v_new = beta_two * v_old[owner] + (1.0 - beta_two) * grad * grad
        m_out[owner] = m_new
        v_out[owner] = v_new
        value = m_new / fixes[0] / (jnp.sqrt(v_new / fixes[1]) + adam_eps)
        update[owner] = value
        update[OWNERS + owner] = value


def adam(fixes, grads, m_old, v_old):
    return pl.pallas_call(
        adam_kernel,
        in_specs=[SMEM] + [VMEM] * 3,
        out_specs=[VMEM] * 3,
        out_shape=[shape(*m_old.shape), shape(*m_old.shape), shape(2 * OWNERS, *m_old.shape[1:])],
        scratch_shapes=[pltpu.VMEM(m_old.shape, f32)],
        compiler_params=params(),
        cost_estimate=COST,
        name="adam",
    )(fixes, grads, m_old, v_old)


def unturn_kernel(rows, low, high, near, held):
    columns = rows.shape[2]
    for yh in range(N_YH):
        held[:, :columns] = rows[yh * OWNERS : (yh + 1) * OWNERS].reshape(LANES, columns)
        turned = held[...].T
        low[yh] = turned[:BACK]
        high[yh] = turned[BACK : 2 * BACK]
        near[yh] = turned[: 2 * BACK]


def unturn(back):
    columns = back.shape[2]
    return pl.pallas_call(
        unturn_kernel,
        in_specs=[VMEM],
        out_specs=[VMEM] * 3,
        out_shape=[shape(N_YH, width, LANES) for width in (BACK, BACK, columns)],
        scratch_shapes=[pltpu.VMEM((LANES, pl.cdiv(columns, LANES) * LANES), f32)],
        compiler_params=params(),
        cost_estimate=COST,
        name="unturn",
    )(back)


def relayed_kernel(up, down, up_out, down_out):
    up_out[...] = up[0]
    down_out[...] = down[1]


def relayed(up, down):
    return pl.pallas_call(
        relayed_kernel,
        in_specs=[VMEM] * 2,
        out_specs=[VMEM] * 2,
        out_shape=[shape(*up.shape[1:])] * 2,
        compiler_params=params(),
        cost_estimate=COST,
        name="relayed",
    )(up, down)


def gathered_kernel(*refs):
    pieces, out = refs[:-1], refs[-1]
    at = 0
    for piece in pieces:
        tiles = [piece[...]] if len(piece.shape) == 2 else [piece[k] for k in range(piece.shape[0])]
        for tile in tiles:
            out[at] = tile
            at += 1


def gathered(*pieces):
    count = sum(p.shape[0] if p.ndim == 3 else 1 for p in pieces)
    return pl.pallas_call(
        gathered_kernel,
        in_specs=[VMEM] * len(pieces),
        out_specs=VMEM,
        out_shape=shape(count, *pieces[0].shape[-2:]),
        compiler_params=params(),
        cost_estimate=COST,
        name="gathered",
    )(*pieces)


def weight_kernel(spots, place, weight, mine, theirs, *refs):
    out, held, sem = refs[-3:]
    c, z = place[0], place[1]
    half = weight.shape[0] // N_CORE
    width = mine.shape[1]
    stores = []
    for piece, core in ((mine, c), (theirs, 1 - c)):
        for slot, (start, yh, to) in enumerate(spots):
            rows = pl.ds(pl.multiple_of(core * half + start, 8), width)
            lanes = lane_tile(yh, z + to)
            old = weight.at[rows, lanes]
            where = held.at[len(stores)]

            def body(r):
                where[r, :] = old[r, :] - learn_rate * (piece[slot, r, :] + decay_rate * old[r, :])

            each(width, body)
            stores.append(pltpu.make_async_copy(where, out.at[rows, lanes], sem.at[len(stores)]))
            stores[-1].start()
    for store in stores:
        store.wait()


def hold_kernel(source, out, sem):
    copy = pltpu.make_async_copy(source, out, sem)
    copy.start()
    copy.wait()


def hold(array):
    return pl.pallas_call(
        hold_kernel,
        in_specs=[pl.BlockSpec(memory_space=pltpu.HBM)],
        out_specs=VMEM,
        out_shape=shape(*array.shape),
        scratch_shapes=[pltpu.SemaphoreType.DMA],
        compiler_params=params(),
        cost_estimate=COST,
        name="hold",
    )(in_hbm(array))


NEAR = ((0, 0, 0), (0, 1, 0))
SIDES = tuple((at, yh, to) for at in (0, BACK) for to in (3, 1) for yh in range(N_YH)) + ((0, 0, 2), (0, 1, 2))
FAR = ((BACK, 0, 2), (BACK, 1, 2))


def write_weight(place, held, piece, spots, so_far):
    done = [] if so_far is None else [so_far]
    stores = N_CORE * len(spots)
    hbm = pl.BlockSpec(memory_space=pltpu.HBM)
    return pl.pallas_call(
        functools.partial(weight_kernel, spots),
        in_specs=[SMEM] + [VMEM] * 3 + [hbm] * len(done),
        out_specs=hbm,
        out_shape=shape(*held.shape),
        input_output_aliases={4: 0} if done else {},
        scratch_shapes=[pltpu.VMEM((stores, *piece.shape[1:]), f32), pltpu.SemaphoreType.DMA((stores,))],
        compiler_params=params(),
        cost_estimate=COST,
        name="write_weight",
    )(place, held, piece, lax.ppermute(piece, "core", SWAP), *done)


def after(value, *others):
    return lax.optimization_barrier((value, *others))[0]


def shards(weight, grad_parts, m_codes, v_codes, m_absmax, v_absmax, code_m, code_v, step):
    half = weight.shape[1] // N_CORE
    place = jnp.stack([lax.axis_index(a) for a in ("core", "z", "yh")]).astype(jnp.int32)
    grad_t = grad_parts[0].T
    weight_t = weight.T

    send_0 = take(place, in_hbm(grad_t), 0, WIDTH, pl.BlockSpec(memory_space=pltpu.HBM))
    other_0 = lax.ppermute(send_0, "core", SWAP)
    send_1 = take(after(place, send_0), grad_t, WIDTH, WIDTH + FIRST, VMEM)
    up, down, keep_0 = pack(place, grad_t, other_0, half, 0)
    up_0, down_0 = ring(up, down)
    other_1 = lax.ppermute(after(send_1, keep_0), "core", SWAP)
    up, down, keep_1, send, mine = pack_rest(place, grad_t, other_1)
    arrived = lax.ppermute(send, "yh", SWAP)
    up_1, down_1 = ring(up, down)
    up2, down2, across, rest_0, own = relay_pack(place, keep_0, up_0, down_0, mine, arrived)
    across = lax.ppermute(across, "z", ACROSS)
    sums_0 = (rest_0, *ring(up2, down2), own, across)
    up2, down2, rest_1 = relay(after(keep_1, rest_0), up_1, down_1)
    sums_1 = (rest_1, *ring(up2, down2))

    count = step[0].astype(f32)
    fix_one = 1.0 - jnp.power(f32(beta_one), count)
    fix_two = 1.0 - jnp.power(f32(beta_two), count)
    fixes = jnp.stack([fix_one, fix_two])
    olds = old_state(after(m_codes, rest_1), v_codes, m_absmax, v_absmax, code_m, code_v, half)
    sums = lax.optimization_barrier((*sums_0, *sums_1, *olds, fixes))[:8]

    grads = exchange(turn(sums))
    m_new, v_new, update = adam(fixes, grads, *olds)
    pair_0, pair_1, near = unturn(exchange(update))

    up_0, down_0 = ring(pair_0, pair_0)
    up_1, down_1 = ring(pair_1, pair_1)
    held = hold(after(weight_t, near))
    new_weight = write_weight(place, held, near, NEAR, None)
    state = new_state(m_new, v_new, m_codes.shape[0], half)
    up_0, down_0, new_weight, *state = lax.optimization_barrier((up_0, down_0, new_weight, *state))
    up2, down2 = relayed(up_0, down_0)
    up_1, down_1 = lax.optimization_barrier((up_1, down_1, up2))[:2]
    far_0 = ring(up2, down2)
    up2, down2 = relayed(up_1, down_1)
    sides = gathered(up_0, down_0, up_1, after(down_1, up2), *far_0)
    up2, down2 = ring(up2, down2)
    new_weight = write_weight(place, held, sides, SIDES, new_weight)
    up2, down2, new_weight = lax.optimization_barrier((up2, down2, new_weight))
    new_weight = write_weight(place, held, gathered(up2, down2), FAR, new_weight)
    return (new_weight.T, *state)


def solution(mesh):
    fine = Mesh(mesh.devices.reshape(N_YH, N_Z, N_CORE, N_YL, N_X), AXES)
    blocks = P(DP + TENSOR)
    in_specs = (P(None, TENSOR), P(DP, None, TENSOR), blocks, blocks, blocks, blocks, P(), P(), P())
    out_specs = (P(None, TENSOR), blocks, blocks, blocks, blocks)
    return jax.shard_map(shards, mesh=fine, in_specs=in_specs, out_specs=out_specs, check_vma=False)
```

```python
import functools

import jax
import jax.numpy as jnp
from jax import lax
from jax.experimental import pallas as pl
from jax.experimental.pallas import tpu as pltpu
from jax.sharding import Mesh, PartitionSpec as P

BLOCK = 2048
LANES = 128
N_YH, N_Z, N_CORE, N_YL, N_X = 2, 4, 2, 2, 4
N_TENSOR = N_YL * N_X
OWNERS = N_CORE * N_TENSOR
AXES = ("yh", "z", "core", "yl", "x")
DP = ("yh", "z", "core")
TENSOR = ("yl", "x")
ROW_OWNERS = ("yh", "core", "yl", "x")
WIDTH = 400
BACK = 496
FIRST = 192
HALF = FIRST // 2
PLAIN = 2 * WIDTH
SENT = PLAIN + HALF

beta_one = 0.9
beta_two = 0.999
adam_eps = 1e-08
learn_rate = 0.02
decay_rate = 0.1
scale_eps = 1e-06

SWAP = [(0, 1), (1, 0)]
UP = [(i, (i + 1) % N_Z) for i in range(N_Z)]
DOWN = [(i, (i - 1) % N_Z) for i in range(N_Z)]
ROUND = [(i * N_CORE + c, (i + (1, -1)[c]) % N_Z * N_CORE + c) for i in range(N_Z) for c in range(N_CORE)]
ACROSS = [(i, (i + 2) % N_Z) for i in range(N_Z)]

ANY = pl.BlockSpec(memory_space=pl.ANY)
SMEM = pl.BlockSpec(memory_space=pltpu.SMEM)
VMEM = pl.BlockSpec(memory_space=pltpu.VMEM)
f32 = jnp.float32
COST = pl.CostEstimate(flops=1, bytes_accessed=1024, transcendentals=0)


def shape(*dims):
    return jax.ShapeDtypeStruct(dims, f32)


def params():
    return pltpu.CompilerParams(vmem_limit_bytes=10 * 2**20)


def lane_tile(yh, z):
    return pl.ds(pl.multiple_of((yh * N_Z + lax.rem(z, N_Z)) * LANES, LANES), LANES)


def each(count, body):
    for r in range(0, count, 8):
        body(slice(r, r + 8))


def segments(rows, row):
    for r in range(rows):
        at = r * row
        while at < (r + 1) * row:
            end = min((r + 1) * row, (at // BLOCK + 1) * BLOCK)
            b = at // BLOCK
            yield r, slice(at - r * row, end - r * row), b, slice(at - b * BLOCK, end - b * BLOCK)
            at = end


def owned(half, owner):
    c, j = divmod(owner, N_TENSOR)
    at = j * N_CORE * half + c * half
    return slice(at, at + half)


def old_state_kernel(half, m_codes, v_codes, m_scale, v_scale, code_m, code_v, m_out, v_out, held, flat):
    outs = (m_out, v_out)
    blocks = m_codes.shape[0]
    for which, (codes, scale, table) in enumerate(((m_codes, m_scale, code_m), (v_codes, v_scale, code_v))):
        low = jnp.broadcast_to(table[0:1, :], (8, LANES))
        high = jnp.broadcast_to(table[1:2, :], (8, LANES))
        for r in range(0, blocks, 8):
            rows = slice(min(r, blocks - 8), min(r, blocks - 8) + 8)
            for k in range(0, BLOCK, LANES):
                index = codes[rows, k : k + LANES]
                lane = index & (LANES - 1)
                a = jnp.take_along_axis(low, lane, axis=1)
                b = jnp.take_along_axis(high, lane, axis=1)
                held[rows, k : k + LANES] = jnp.where(index < LANES, a, b)
        for r, columns, b, inside in segments(*flat.shape):
            flat[r : r + 1, columns] = held[b : b + 1, inside] * scale[b]
        for owner in range(OWNERS):
            outs[which][owner] = flat[:, owned(half, owner)]


def old_state(m_codes, v_codes, m_absmax, v_absmax, code_m, code_v, half):
    rows = LANES // OWNERS
    return pl.pallas_call(
        functools.partial(old_state_kernel, half),
        in_specs=[VMEM, VMEM, SMEM, SMEM, VMEM, VMEM],
        out_specs=[VMEM] * 2,
        out_shape=[shape(OWNERS, rows, half)] * 2,
        scratch_shapes=[pltpu.VMEM(m_codes.shape, f32), pltpu.VMEM((rows, N_CORE * half * N_TENSOR), f32)],
        compiler_params=params(),
        cost_estimate=COST,
        name="old_state",
    )(m_codes, v_codes, m_absmax, v_absmax, code_m.reshape(2, LANES), code_v.reshape(2, LANES))


def new_state_kernel(half, m_in, v_in, *refs):
    outs, (held, flat) = refs[:4], refs[4:]
    blocks = outs[0].shape[0]
    for which, values in enumerate((m_in, v_in)):
        for owner in range(OWNERS):
            flat[:, owned(half, owner)] = values[owner]
        for r, columns, b, inside in segments(*flat.shape):
            held[b : b + 1, inside] = flat[r : r + 1, columns]
        value = held[...]
        largest = jnp.max(jnp.abs(value) if which == 0 else value, axis=1, keepdims=True)
        outs[which][...] = (value / (largest + scale_eps)).astype(jnp.bfloat16)[:blocks]
        outs[2 + which][...] = jnp.broadcast_to(largest, (held.shape[0], LANES)).T[0:1, :blocks]


def new_state(m_new, v_new, blocks, half):
    rows = LANES // OWNERS
    scaled = jax.ShapeDtypeStruct((blocks, BLOCK), jnp.bfloat16)
    m_scaled, v_scaled, m_absmax, v_absmax = pl.pallas_call(
        functools.partial(new_state_kernel, half),
        in_specs=[VMEM] * 2,
        out_specs=[VMEM] * 4,
        out_shape=[scaled, scaled, shape(1, blocks), shape(1, blocks)],
        scratch_shapes=[
            pltpu.VMEM((pl.cdiv(blocks, 8) * 8, BLOCK), f32),
            pltpu.VMEM((rows, N_CORE * half * N_TENSOR), f32),
        ],
        compiler_params=params(),
        cost_estimate=COST,
        name="new_state",
    )(m_new, v_new)
    return m_scaled, v_scaled, m_absmax[0], v_absmax[0]


def in_hbm(array):
    return pltpu.with_memory_space_constraint(array, pltpu.HBM)


def columns_at(core, half, start, width):
    return pl.ds(pl.multiple_of(core * half + start, 8), width)


def take_kernel(half, start, place, source, send, sem):
    rows = columns_at(1 - place[0], half, start, send.shape[0])
    copy = pltpu.make_async_copy(source.at[rows], send, sem)
    copy.start()
    copy.wait()


def take(place, source, start, width, spec):
    return pl.pallas_call(
        functools.partial(take_kernel, source.shape[0] // N_CORE, start),
        in_specs=[SMEM, spec],
        out_specs=VMEM,
        out_shape=shape(width, source.shape[1]),
        scratch_shapes=[pltpu.SemaphoreType.DMA],
        compiler_params=params(),
        cost_estimate=COST,
        name="take_part",
    )(place, source)


def pack_tiles(place, source, base, other, up, down, keep):
    z = place[1]
    rows = other.shape[0]
    for out, slot, yh, to in (
        (up, 0, 0, 2),
        (down, 0, 1, 2),
        (up, 1, 1, 1),
        (down, 1, 0, 3),
        (keep, 0, 0, 1),
        (keep, 1, 1, 3),
        (keep, 2, 0, 0),
        (keep, 3, 1, 0),
    ):
        lanes = lane_tile(yh, z + to)
        one = source.at[pl.ds(pl.multiple_of(base, 8), rows), lanes]
        two = other.at[:, lanes]

        def body(r):
            out[slot, r, :] = one[r, :] + two[r, :]

        each(rows, body)


def pack_kernel(half, start, place, source, other, up, down, keep):
    pack_tiles(place, source, place[0] * half + start, other, up, down, keep)


def packed(width):
    return [shape(n, width, LANES) for n in (2, 2, 4)]


def pack(place, source, other, half, start):
    return pl.pallas_call(
        functools.partial(pack_kernel, half, start),
        in_specs=[SMEM, VMEM, VMEM],
        out_specs=[VMEM] * 3,
        out_shape=packed(other.shape[0]),
        compiler_params=params(),
        cost_estimate=COST,
        name="pack",
    )(place, source, other)


def pack_rest_kernel(half, place, grad, other, up, down, keep, send, mine):
    c, yh = place[0], place[2]
    for out, which in ((send, 1 - yh), (mine, yh)):
        at = which * HALF
        one = grad.at[pl.ds(pl.multiple_of(c * half + PLAIN + at, 8), HALF)]
        two = other.at[pl.ds(pl.multiple_of(WIDTH + at, 8), HALF)]

        def body(r):
            out[r, :] = one[r, :] + two[r, :]

        each(HALF, body)
    pack_tiles(place, grad, c * half + WIDTH, other.at[:WIDTH], up, down, keep)


def pack_rest(place, grad_t, other):
    return pl.pallas_call(
        functools.partial(pack_rest_kernel, grad_t.shape[0] // N_CORE),
        in_specs=[SMEM, VMEM, VMEM],
        out_specs=[VMEM] * 5,
        out_shape=packed(WIDTH) + [shape(HALF, grad_t.shape[1])] * 2,
        compiler_params=params(),
        cost_estimate=COST,
        name="pack_rest",
    )(place, grad_t, other)


def relay_kernel(keep, up, down, up2, down2, rest):
    def body(r):
        up2[r, :] = keep[0, r, :] + up[0, r, :]
        down2[r, :] = keep[1, r, :] + down[0, r, :]
        rest[0, r, :] = keep[2, r, :] + down[1, r, :]
        rest[1, r, :] = keep[3, r, :] + up[1, r, :]

    each(keep.shape[1], body)


def relay(keep, up, down):
    tile = keep.shape[1:]
    return pl.pallas_call(
        relay_kernel,
        in_specs=[VMEM] * 3,
        out_specs=[VMEM] * 3,
        out_shape=[shape(*tile), shape(*tile), shape(N_YH, *tile)],
        compiler_params=params(),
        cost_estimate=COST,
        name="relay",
    )(keep, up, down)


def relay_pack_kernel(place, keep, up, down, mine, arrived, up2, down2, across, rest, own):
    z = place[1]

    def body(r):
        up2[r, :] = keep[0, r, :] + up[0, r, :]
        down2[r, :] = keep[1, r, :] + down[0, r, :]
        rest[0, r, :] = keep[2, r, :] + down[1, r, :]
        rest[1, r, :] = keep[3, r, :] + up[1, r, :]

    each(WIDTH, body)
    for yh in range(N_YH):
        part = pl.ds(WIDTH + yh * HALF, HALF)
        for out, to in ((own.at[yh], 0), (up2.at[part], 1), (across.at[yh], 2), (down2.at[part], 3)):
            lanes = lane_tile(yh, z + to)
            one, two = mine.at[:, lanes], arrived.at[:, lanes]

            def third(r):
                out[r, :] = one[r, :] + two[r, :]

            each(HALF, third)


def relay_pack(place, keep, up, down, mine, arrived):
    sent = shape(WIDTH + N_YH * HALF, LANES)
    third = shape(N_YH, HALF, LANES)
    return pl.pallas_call(
        relay_pack_kernel,
        in_specs=[SMEM] + [VMEM] * 5,
        out_specs=[VMEM] * 5,
        out_shape=[sent, sent, third, shape(N_YH, WIDTH, LANES), third],
        compiler_params=params(),
        cost_estimate=COST,
        name="relay_pack",
    )(place, keep, up, down, mine, arrived)


def ring(up, down):
    return lax.ppermute(up, "z", UP), lax.ppermute(down, "z", DOWN)


def turn_kernel(rest_0, up_0, down_0, own, across, rest_1, up_1, down_1, out, held):
    for yh in range(N_YH):
        low, high = ((up_0, up_1), (down_0, down_1))[yh]
        held[:WIDTH, :] = rest_0[yh] + low[:WIDTH, :]
        held[WIDTH:PLAIN, :] = rest_1[yh] + high[...]
        part = pl.ds(WIDTH + yh * HALF, HALF)
        held[PLAIN:SENT, :] = own[yh] + up_0[part, :] + down_0[part, :] + across[yh]
        out[yh * OWNERS : (yh + 1) * OWNERS] = held[...].T[:, :SENT].reshape(OWNERS, -1, SENT)


def turn(sums):
    return pl.pallas_call(
        turn_kernel,
        in_specs=[VMEM] * len(sums),
        out_specs=VMEM,
        out_shape=shape(N_YH * OWNERS, LANES // OWNERS, SENT),
        scratch_shapes=[pltpu.VMEM((pl.cdiv(SENT, LANES) * LANES, LANES), f32)],
        compiler_params=params(),
        cost_estimate=COST,
        name="turn",
    )(*sums)


def exchange(array):
    return lax.all_to_all(array, ROW_OWNERS, split_axis=0, concat_axis=0, tiled=True)


def adam_kernel(fixes, grads, m_old, v_old, m_out, v_out, update, held):
    for owner in range(OWNERS):
        held[owner, :, :SENT] = grads[owner]
        held[owner, :, :PLAIN] += grads[OWNERS + owner, :, :PLAIN]
        held[owner, :, SENT:] = grads[OWNERS + owner, :, PLAIN:]
        grad = held[owner]
        m_new = beta_one * m_old[owner] + (1.0 - beta_one) * grad
        v_new = beta_two * v_old[owner] + (1.0 - beta_two) * grad * grad
        m_out[owner] = m_new
        v_out[owner] = v_new
        value = m_new / fixes[0] / (jnp.sqrt(v_new / fixes[1]) + adam_eps)
        update[owner] = value
        update[OWNERS + owner] = value


def adam(fixes, grads, m_old, v_old):
    return pl.pallas_call(
        adam_kernel,
        in_specs=[SMEM] + [VMEM] * 3,
        out_specs=[VMEM] * 3,
        out_shape=[shape(*m_old.shape), shape(*m_old.shape), shape(2 * OWNERS, *m_old.shape[1:])],
        scratch_shapes=[pltpu.VMEM(m_old.shape, f32)],
        compiler_params=params(),
        cost_estimate=COST,
        name="adam",
    )(fixes, grads, m_old, v_old)


def unturn_kernel(rows, low, high, near, held):
    columns = rows.shape[2]
    for yh in range(N_YH):
        held[:, :columns] = rows[yh * OWNERS : (yh + 1) * OWNERS].reshape(LANES, columns)
        turned = held[...].T
        low[yh] = turned[:BACK]
        high[yh] = turned[BACK : 2 * BACK]
        near[yh] = turned[: 2 * BACK]


def unturn(back):
    columns = back.shape[2]
    return pl.pallas_call(
        unturn_kernel,
        in_specs=[VMEM],
        out_specs=[VMEM] * 3,
        out_shape=[shape(N_YH, width, LANES) for width in (BACK, BACK, columns)],
        scratch_shapes=[pltpu.VMEM((LANES, pl.cdiv(columns, LANES) * LANES), f32)],
        compiler_params=params(),
        cost_estimate=COST,
        name="unturn",
    )(back)


def weight_kernel(spots, place, weight, *refs):
    pieces, (out, held, sem) = refs[: 2 * len(spots)], refs[-3:]
    c, z = place[0], place[1]
    half = weight.shape[0] // N_CORE
    stores = []
    for k, piece in enumerate(pieces):
        core = c if k < len(spots) else 1 - c
        start, steps = spots[k % len(spots)]
        width = piece.shape[1]
        rows = pl.ds(pl.multiple_of(core * half + start, 8), width)
        for yh in range(N_YH):
            lanes = lane_tile(yh, z + steps + (1 - core) * (N_Z - 2 * steps))
            old = weight.at[rows, lanes]
            where = held.at[len(stores)]

            def body(r):
                where[r, :] = old[r, :] - learn_rate * (piece[yh, r, :] + decay_rate * old[r, :])

            each(width, body)
            stores.append(pltpu.make_async_copy(where, out.at[rows, lanes], sem.at[len(stores)]))
            stores[-1].start()
    for store in stores:
        store.wait()


def hold_kernel(source, out, sem):
    copy = pltpu.make_async_copy(source, out, sem)
    copy.start()
    copy.wait()


def hold(array):
    return pl.pallas_call(
        hold_kernel,
        in_specs=[pl.BlockSpec(memory_space=pltpu.HBM)],
        out_specs=VMEM,
        out_shape=shape(*array.shape),
        scratch_shapes=[pltpu.SemaphoreType.DMA],
        compiler_params=params(),
        cost_estimate=COST,
        name="hold",
    )(in_hbm(array))


def write_weight(place, held, pieces, spots, so_far):
    done = [] if so_far is None else [so_far]
    pieces = list(pieces) + [lax.ppermute(p, "core", SWAP) for p in pieces]
    stores = N_YH * len(pieces)
    hbm = pl.BlockSpec(memory_space=pltpu.HBM)
    return pl.pallas_call(
        functools.partial(weight_kernel, spots),
        in_specs=[SMEM] + [VMEM] * (1 + len(pieces)) + [hbm] * len(done),
        out_specs=hbm,
        out_shape=shape(*held.shape),
        input_output_aliases={2 + len(pieces): 0} if done else {},
        scratch_shapes=[pltpu.VMEM((stores, *pieces[0].shape[1:]), f32), pltpu.SemaphoreType.DMA((stores,))],
        compiler_params=params(),
        cost_estimate=COST,
        name="write_weight",
    )(place, held, *pieces, *done)


def after(value, *others):
    return lax.optimization_barrier((value, *others))[0]


def shards(weight, grad_parts, m_codes, v_codes, m_absmax, v_absmax, code_m, code_v, step):
    half = weight.shape[1] // N_CORE
    place = jnp.stack([lax.axis_index(a) for a in ("core", "z", "yh")]).astype(jnp.int32)
    grad_t = grad_parts[0].T
    weight_t = weight.T

    send_0 = take(place, in_hbm(grad_t), 0, WIDTH, pl.BlockSpec(memory_space=pltpu.HBM))
    other_0 = lax.ppermute(send_0, "core", SWAP)
    send_1 = take(after(place, send_0), grad_t, WIDTH, WIDTH + FIRST, VMEM)
    up, down, keep_0 = pack(place, grad_t, other_0, half, 0)
    up_0, down_0 = ring(up, down)
    other_1 = lax.ppermute(after(send_1, keep_0), "core", SWAP)
    up, down, keep_1, send, mine = pack_rest(place, grad_t, other_1)
    arrived = lax.ppermute(send, "yh", SWAP)
    up_1, down_1 = ring(up, down)
    up2, down2, across, rest_0, own = relay_pack(place, keep_0, up_0, down_0, mine, arrived)
    across = lax.ppermute(across, "z", ACROSS)
    sums_0 = (rest_0, *ring(up2, down2), own, across)
    up2, down2, rest_1 = relay(after(keep_1, rest_0), up_1, down_1)
    sums_1 = (rest_1, *ring(up2, down2))

    count = step[0].astype(f32)
    fix_one = 1.0 - jnp.power(f32(beta_one), count)
    fix_two = 1.0 - jnp.power(f32(beta_two), count)
    fixes = jnp.stack([fix_one, fix_two])
    olds = old_state(after(m_codes, rest_1), v_codes, m_absmax, v_absmax, code_m, code_v, half)
    sums = lax.optimization_barrier((*sums_0, *sums_1, *olds, fixes))[:8]

    grads = exchange(turn(sums))
    m_new, v_new, update = adam(fixes, grads, *olds)
    pair_0, pair_1, near = unturn(exchange(update))

    def step(piece):
        return lax.ppermute(piece, ("z", "core"), ROUND)

    low_1, high_1 = step(pair_0), step(pair_1)
    held = hold(after(weight_t, near))
    new_weight = write_weight(place, held, (near,), ((0, 0),), None)
    state = new_state(m_new, v_new, m_codes.shape[0], half)
    low_1, new_weight, *state = lax.optimization_barrier((low_1, new_weight, *state))
    low_2, high_2 = step(low_1), step(high_1)
    low_3, high_3 = step(low_2), step(high_2)
    pieces = lax.optimization_barrier((low_1, high_1, new_weight))
    new_weight = write_weight(place, held, pieces[:2], ((0, 1), (BACK, 1)), pieces[2])
    pieces = lax.optimization_barrier((low_2, high_2, low_3, high_3, new_weight))
    new_weight = write_weight(place, held, pieces[:2], ((0, 2), (BACK, 2)), pieces[4])
    new_weight = write_weight(place, held, pieces[2:4], ((0, 3), (BACK, 3)), new_weight)
    return (new_weight.T, *state)


def solution(mesh):
    fine = Mesh(mesh.devices.reshape(N_YH, N_Z, N_CORE, N_YL, N_X), AXES)
    blocks = P(DP + TENSOR)
    in_specs = (P(None, TENSOR), P(DP, None, TENSOR), blocks, blocks, blocks, blocks, P(), P(), P())
    out_specs = (P(None, TENSOR), blocks, blocks, blocks, blocks)
    return jax.shard_map(shards, mesh=fine, in_specs=in_specs, out_specs=out_specs, check_vma=False)
```

```python
import functools

import jax
import jax.numpy as jnp
from jax import lax
from jax.experimental import pallas as pl
from jax.experimental.pallas import tpu as pltpu
from jax.sharding import Mesh, PartitionSpec as P

BLOCK = 2048
LANES = 128
N_YH, N_Z, N_CORE, N_YL, N_X = 2, 4, 2, 2, 4
N_TENSOR = N_YL * N_X
OWNERS = N_CORE * N_TENSOR
AXES = ("yh", "z", "core", "yl", "x")
DP = ("yh", "z", "core")
TENSOR = ("yl", "x")
ROW_OWNERS = ("yh", "core", "yl", "x")
WIDTH = 400
BACK = 496
FIRST = 192
HALF = FIRST // 2
PLAIN = 2 * WIDTH
SENT = PLAIN + HALF

beta_one = 0.9
beta_two = 0.999
adam_eps = 1e-08
learn_rate = 0.02
decay_rate = 0.1
scale_eps = 1e-06

SWAP = [(0, 1), (1, 0)]
UP = [(i, (i + 1) % N_Z) for i in range(N_Z)]
DOWN = [(i, (i - 1) % N_Z) for i in range(N_Z)]
ROUND = [(i * N_CORE + c, (i + (1, -1)[c]) % N_Z * N_CORE + c) for i in range(N_Z) for c in range(N_CORE)]
ACROSS = [(i, (i + 2) % N_Z) for i in range(N_Z)]

ANY = pl.BlockSpec(memory_space=pl.ANY)
SMEM = pl.BlockSpec(memory_space=pltpu.SMEM)
VMEM = pl.BlockSpec(memory_space=pltpu.VMEM)
f32 = jnp.float32
COST = pl.CostEstimate(flops=1, bytes_accessed=1024, transcendentals=0)


def shape(*dims):
    return jax.ShapeDtypeStruct(dims, f32)


def params():
    return pltpu.CompilerParams(vmem_limit_bytes=10 * 2**20)


def lane_tile(yh, z):
    return pl.ds(pl.multiple_of((yh * N_Z + lax.rem(z, N_Z)) * LANES, LANES), LANES)


def each(count, body):
    for r in range(0, count, 8):
        body(slice(r, r + 8))


def segments(rows, row):
    for r in range(rows):
        at = r * row
        while at < (r + 1) * row:
            end = min((r + 1) * row, (at // BLOCK + 1) * BLOCK)
            b = at // BLOCK
            yield r, slice(at - r * row, end - r * row), b, slice(at - b * BLOCK, end - b * BLOCK)
            at = end


def owned(half, owner):
    c, j = divmod(owner, N_TENSOR)
    at = j * N_CORE * half + c * half
    return slice(at, at + half)


def old_state_kernel(half, m_codes, v_codes, m_scale, v_scale, code_m, code_v, m_out, v_out, held, flat):
    outs = (m_out, v_out)
    blocks = m_codes.shape[0]
    for which, (codes, scale, table) in enumerate(((m_codes, m_scale, code_m), (v_codes, v_scale, code_v))):
        low = jnp.broadcast_to(table[0:1, :], (8, LANES))
        high = jnp.broadcast_to(table[1:2, :], (8, LANES))
        for r in range(0, blocks, 8):
            rows = slice(min(r, blocks - 8), min(r, blocks - 8) + 8)
            for k in range(0, BLOCK, LANES):
                index = codes[rows, k : k + LANES]
                lane = index & (LANES - 1)
                a = jnp.take_along_axis(low, lane, axis=1)
                b = jnp.take_along_axis(high, lane, axis=1)
                held[rows, k : k + LANES] = jnp.where(index < LANES, a, b)
        for r, columns, b, inside in segments(*flat.shape):
            flat[r : r + 1, columns] = held[b : b + 1, inside] * scale[b]
        for owner in range(OWNERS):
            outs[which][owner] = flat[:, owned(half, owner)]


def old_state(m_codes, v_codes, m_absmax, v_absmax, code_m, code_v, half):
    rows = LANES // OWNERS
    return pl.pallas_call(
        functools.partial(old_state_kernel, half),
        in_specs=[VMEM, VMEM, SMEM, SMEM, VMEM, VMEM],
        out_specs=[VMEM] * 2,
        out_shape=[shape(OWNERS, rows, half)] * 2,
        scratch_shapes=[pltpu.VMEM(m_codes.shape, f32), pltpu.VMEM((rows, N_CORE * half * N_TENSOR), f32)],
        compiler_params=params(),
        cost_estimate=COST,
        name="old_state",
    )(m_codes, v_codes, m_absmax, v_absmax, code_m.reshape(2, LANES), code_v.reshape(2, LANES))


def new_state_kernel(half, m_in, v_in, *refs):
    outs, (held, flat) = refs[:4], refs[4:]
    blocks = outs[0].shape[0]
    for which, values in enumerate((m_in, v_in)):
        for owner in range(OWNERS):
            flat[:, owned(half, owner)] = values[owner]
        for r, columns, b, inside in segments(*flat.shape):
            held[b : b + 1, inside] = flat[r : r + 1, columns]
        value = held[...]
        largest = jnp.max(jnp.abs(value) if which == 0 else value, axis=1, keepdims=True)
        outs[which][...] = (value / (largest + scale_eps)).astype(jnp.bfloat16)[:blocks]
        outs[2 + which][...] = jnp.broadcast_to(largest, (held.shape[0], LANES)).T[0:1, :blocks]


def new_state(m_new, v_new, blocks, half):
    rows = LANES // OWNERS
    scaled = jax.ShapeDtypeStruct((blocks, BLOCK), jnp.bfloat16)
    m_scaled, v_scaled, m_absmax, v_absmax = pl.pallas_call(
        functools.partial(new_state_kernel, half),
        in_specs=[VMEM] * 2,
        out_specs=[VMEM] * 4,
        out_shape=[scaled, scaled, shape(1, blocks), shape(1, blocks)],
        scratch_shapes=[
            pltpu.VMEM((pl.cdiv(blocks, 8) * 8, BLOCK), f32),
            pltpu.VMEM((rows, N_CORE * half * N_TENSOR), f32),
        ],
        compiler_params=params(),
        cost_estimate=COST,
        name="new_state",
    )(m_new, v_new)
    return m_scaled, v_scaled, m_absmax[0], v_absmax[0]


def in_hbm(array):
    return pltpu.with_memory_space_constraint(array, pltpu.HBM)


def columns_at(core, half, start, width):
    return pl.ds(pl.multiple_of(core * half + start, 8), width)


def take_kernel(half, start, place, source, send, sem):
    rows = columns_at(1 - place[0], half, start, send.shape[0])
    copy = pltpu.make_async_copy(source.at[rows], send, sem)
    copy.start()
    copy.wait()


def take(place, source, start, width, spec):
    return pl.pallas_call(
        functools.partial(take_kernel, source.shape[0] // N_CORE, start),
        in_specs=[SMEM, spec],
        out_specs=VMEM,
        out_shape=shape(width, source.shape[1]),
        scratch_shapes=[pltpu.SemaphoreType.DMA],
        compiler_params=params(),
        cost_estimate=COST,
        name="take_part",
    )(place, source)


def pack_tiles(place, source, base, other, up, down, keep):
    z = place[1]
    rows = other.shape[0]
    for out, slot, yh, to in (
        (up, 0, 0, 2),
        (down, 0, 1, 2),
        (up, 1, 1, 1),
        (down, 1, 0, 3),
        (keep, 0, 0, 1),
        (keep, 1, 1, 3),
        (keep, 2, 0, 0),
        (keep, 3, 1, 0),
    ):
        lanes = lane_tile(yh, z + to)
        one = source.at[pl.ds(pl.multiple_of(base, 8), rows), lanes]
        two = other.at[:, lanes]

        def body(r):
            out[slot, r, :] = one[r, :] + two[r, :]

        each(rows, body)


def pack_kernel(half, start, place, source, other, up, down, keep):
    pack_tiles(place, source, place[0] * half + start, other, up, down, keep)


def packed(width):
    return [shape(n, width, LANES) for n in (2, 2, 4)]


def pack(place, source, other, half, start):
    return pl.pallas_call(
        functools.partial(pack_kernel, half, start),
        in_specs=[SMEM, VMEM, VMEM],
        out_specs=[VMEM] * 3,
        out_shape=packed(other.shape[0]),
        compiler_params=params(),
        cost_estimate=COST,
        name="pack",
    )(place, source, other)


def pack_rest_kernel(half, place, grad, other, up, down, keep, send, mine):
    c, yh = place[0], place[2]
    for out, which in ((send, 1 - yh), (mine, yh)):
        at = which * HALF
        one = grad.at[pl.ds(pl.multiple_of(c * half + PLAIN + at, 8), HALF)]
        two = other.at[pl.ds(pl.multiple_of(WIDTH + at, 8), HALF)]

        def body(r):
            out[r, :] = one[r, :] + two[r, :]

        each(HALF, body)
    pack_tiles(place, grad, c * half + WIDTH, other.at[:WIDTH], up, down, keep)


def pack_rest(place, grad_t, other):
    return pl.pallas_call(
        functools.partial(pack_rest_kernel, grad_t.shape[0] // N_CORE),
        in_specs=[SMEM, VMEM, VMEM],
        out_specs=[VMEM] * 5,
        out_shape=packed(WIDTH) + [shape(HALF, grad_t.shape[1])] * 2,
        compiler_params=params(),
        cost_estimate=COST,
        name="pack_rest",
    )(place, grad_t, other)


def relay_kernel(keep, up, down, up2, down2, rest):
    def body(r):
        up2[r, :] = keep[0, r, :] + up[0, r, :]
        down2[r, :] = keep[1, r, :] + down[0, r, :]
        rest[0, r, :] = keep[2, r, :] + down[1, r, :]
        rest[1, r, :] = keep[3, r, :] + up[1, r, :]

    each(keep.shape[1], body)


def relay(keep, up, down):
    tile = keep.shape[1:]
    return pl.pallas_call(
        relay_kernel,
        in_specs=[VMEM] * 3,
        out_specs=[VMEM] * 3,
        out_shape=[shape(*tile), shape(*tile), shape(N_YH, *tile)],
        compiler_params=params(),
        cost_estimate=COST,
        name="relay",
    )(keep, up, down)


def relay_pack_kernel(place, keep, up, down, mine, arrived, up2, down2, across, rest, own):
    z = place[1]

    def body(r):
        up2[r, :] = keep[0, r, :] + up[0, r, :]
        down2[r, :] = keep[1, r, :] + down[0, r, :]
        rest[0, r, :] = keep[2, r, :] + down[1, r, :]
        rest[1, r, :] = keep[3, r, :] + up[1, r, :]

    each(WIDTH, body)
    for yh in range(N_YH):
        part = pl.ds(WIDTH + yh * HALF, HALF)
        for out, to in ((own.at[yh], 0), (up2.at[part], 1), (across.at[yh], 2), (down2.at[part], 3)):
            lanes = lane_tile(yh, z + to)
            one, two = mine.at[:, lanes], arrived.at[:, lanes]

            def third(r):
                out[r, :] = one[r, :] + two[r, :]

            each(HALF, third)


def relay_pack(place, keep, up, down, mine, arrived):
    sent = shape(WIDTH + N_YH * HALF, LANES)
    third = shape(N_YH, HALF, LANES)
    return pl.pallas_call(
        relay_pack_kernel,
        in_specs=[SMEM] + [VMEM] * 5,
        out_specs=[VMEM] * 5,
        out_shape=[sent, sent, third, shape(N_YH, WIDTH, LANES), third],
        compiler_params=params(),
        cost_estimate=COST,
        name="relay_pack",
    )(place, keep, up, down, mine, arrived)


def ring(up, down):
    return lax.ppermute(up, "z", UP), lax.ppermute(down, "z", DOWN)


def turn_kernel(rest_0, up_0, down_0, own, across, rest_1, up_1, down_1, out, held):
    for yh in range(N_YH):
        low, high = ((up_0, up_1), (down_0, down_1))[yh]
        held[:WIDTH, :] = rest_0[yh] + low[:WIDTH, :]
        held[WIDTH:PLAIN, :] = rest_1[yh] + high[...]
        part = pl.ds(WIDTH + yh * HALF, HALF)
        held[PLAIN:SENT, :] = own[yh] + up_0[part, :] + down_0[part, :] + across[yh]
        out[yh * OWNERS : (yh + 1) * OWNERS] = held[...].T[:, :SENT].reshape(OWNERS, -1, SENT)


def turn(sums):
    return pl.pallas_call(
        turn_kernel,
        in_specs=[VMEM] * len(sums),
        out_specs=VMEM,
        out_shape=shape(N_YH * OWNERS, LANES // OWNERS, SENT),
        scratch_shapes=[pltpu.VMEM((pl.cdiv(SENT, LANES) * LANES, LANES), f32)],
        compiler_params=params(),
        cost_estimate=COST,
        name="turn",
    )(*sums)


def exchange(array):
    return lax.all_to_all(array, ROW_OWNERS, split_axis=0, concat_axis=0, tiled=True)


def adam_kernel(fixes, grads, m_old, v_old, m_out, v_out, update, held):
    for owner in range(OWNERS):
        held[owner, :, :SENT] = grads[owner]
        held[owner, :, :PLAIN] += grads[OWNERS + owner, :, :PLAIN]
        held[owner, :, SENT:] = grads[OWNERS + owner, :, PLAIN:]
        grad = held[owner]
        m_new = beta_one * m_old[owner] + (1.0 - beta_one) * grad
        v_new = beta_two * v_old[owner] + (1.0 - beta_two) * grad * grad
        m_out[owner] = m_new
        v_out[owner] = v_new
        value = m_new / fixes[0] / (jnp.sqrt(v_new / fixes[1]) + adam_eps)
        update[owner] = value
        update[OWNERS + owner] = value


def adam(fixes, grads, m_old, v_old):
    return pl.pallas_call(
        adam_kernel,
        in_specs=[SMEM] + [VMEM] * 3,
        out_specs=[VMEM] * 3,
        out_shape=[shape(*m_old.shape), shape(*m_old.shape), shape(2 * OWNERS, *m_old.shape[1:])],
        scratch_shapes=[pltpu.VMEM(m_old.shape, f32)],
        compiler_params=params(),
        cost_estimate=COST,
        name="adam",
    )(fixes, grads, m_old, v_old)


def unturn_kernel(rows, low, high, near, held):
    columns = rows.shape[2]
    for yh in range(N_YH):
        held[:, :columns] = rows[yh * OWNERS : (yh + 1) * OWNERS].reshape(LANES, columns)
        turned = held[...].T
        low[yh] = turned[:BACK]
        high[yh] = turned[BACK : 2 * BACK]
        near[yh] = turned[: 2 * BACK]


def unturn(back):
    columns = back.shape[2]
    return pl.pallas_call(
        unturn_kernel,
        in_specs=[VMEM],
        out_specs=[VMEM] * 3,
        out_shape=[shape(N_YH, width, LANES) for width in (BACK, BACK, columns)],
        scratch_shapes=[pltpu.VMEM((LANES, pl.cdiv(columns, LANES) * LANES), f32)],
        compiler_params=params(),
        cost_estimate=COST,
        name="unturn",
    )(back)


def weight_kernel(spots, place, weight, *refs):
    pieces, (out, held, sem) = refs[: len(spots)], refs[-3:]
    c, z = place[0], place[1]
    half = weight.shape[0] // N_CORE
    stores = []
    for k, piece in enumerate(pieces):
        own, start, steps = spots[k]
        core = c if own else 1 - c
        width = piece.shape[1]
        rows = pl.ds(pl.multiple_of(core * half + start, 8), width)
        for yh in range(N_YH):
            lanes = lane_tile(yh, z + steps + (1 - core) * (N_Z - 2 * steps))
            old = weight.at[rows, lanes]
            where = held.at[len(stores)]

            def body(r):
                where[r, :] = old[r, :] - learn_rate * (piece[yh, r, :] + decay_rate * old[r, :])

            each(width, body)
            stores.append(pltpu.make_async_copy(where, out.at[rows, lanes], sem.at[len(stores)]))
            stores[-1].start()
    for store in stores:
        store.wait()


def hold_kernel(source, out, sem):
    copy = pltpu.make_async_copy(source, out, sem)
    copy.start()
    copy.wait()


def hold(array):
    return pl.pallas_call(
        hold_kernel,
        in_specs=[pl.BlockSpec(memory_space=pltpu.HBM)],
        out_specs=VMEM,
        out_shape=shape(*array.shape),
        scratch_shapes=[pltpu.SemaphoreType.DMA],
        compiler_params=params(),
        cost_estimate=COST,
        name="hold",
    )(in_hbm(array))


def write_weight(place, held, pieces, spots, so_far):
    done = [] if so_far is None else [so_far]
    stores = N_YH * len(pieces)
    hbm = pl.BlockSpec(memory_space=pltpu.HBM)
    return pl.pallas_call(
        functools.partial(weight_kernel, spots),
        in_specs=[SMEM] + [VMEM] * (1 + len(pieces)) + [hbm] * len(done),
        out_specs=hbm,
        out_shape=shape(*held.shape),
        input_output_aliases={2 + len(pieces): 0} if done else {},
        scratch_shapes=[pltpu.VMEM((stores, *pieces[0].shape[1:]), f32), pltpu.SemaphoreType.DMA((stores,))],
        compiler_params=params(),
        cost_estimate=COST,
        name="write_weight",
    )(place, held, *pieces, *done)


def after(value, *others):
    return lax.optimization_barrier((value, *others))[0]


def shards(weight, grad_parts, m_codes, v_codes, m_absmax, v_absmax, code_m, code_v, step):
    half = weight.shape[1] // N_CORE
    place = jnp.stack([lax.axis_index(a) for a in ("core", "z", "yh")]).astype(jnp.int32)
    grad_t = grad_parts[0].T
    weight_t = weight.T

    send_0 = take(place, in_hbm(grad_t), 0, WIDTH, pl.BlockSpec(memory_space=pltpu.HBM))
    other_0 = lax.ppermute(send_0, "core", SWAP)
    send_1 = take(after(place, send_0), grad_t, WIDTH, WIDTH + FIRST, VMEM)
    up, down, keep_0 = pack(place, grad_t, other_0, half, 0)
    up_0, down_0 = ring(up, down)
    other_1 = lax.ppermute(after(send_1, keep_0), "core", SWAP)
    up, down, keep_1, send, mine = pack_rest(place, grad_t, other_1)
    arrived = lax.ppermute(send, "yh", SWAP)
    up_1, down_1 = ring(up, down)
    up2, down2, across, rest_0, own = relay_pack(place, keep_0, up_0, down_0, mine, arrived)
    across = lax.ppermute(across, "z", ACROSS)
    sums_0 = (rest_0, *ring(up2, down2), own, across)
    up2, down2, rest_1 = relay(after(keep_1, rest_0), up_1, down_1)
    sums_1 = (rest_1, *ring(up2, down2))

    count = step[0].astype(f32)
    fix_one = 1.0 - jnp.power(f32(beta_one), count)
    fix_two = 1.0 - jnp.power(f32(beta_two), count)
    fixes = jnp.stack([fix_one, fix_two])
    olds = old_state(after(m_codes, rest_1), v_codes, m_absmax, v_absmax, code_m, code_v, half)
    sums = lax.optimization_barrier((*sums_0, *sums_1, *olds, fixes))[:8]

    grads = exchange(turn(sums))
    m_new, v_new, update = adam(fixes, grads, *olds)
    pair_0, pair_1, near = unturn(exchange(update))

    def swap(piece):
        return lax.ppermute(piece, "core", SWAP)

    def step(piece):
        return lax.ppermute(piece, ("z", "core"), ROUND)

    low_1, high_1 = step(pair_0), step(pair_1)
    held = hold(after(weight_t, near))
    new_weight = write_weight(place, held, (near, swap(near)), ((True, 0, 0), (False, 0, 0)), None)
    state = new_state(m_new, v_new, m_codes.shape[0], half)
    low_1, new_weight, *state = lax.optimization_barrier((low_1, new_weight, *state))
    low_2, high_2 = step(low_1), step(high_1)
    low_3, high_3 = step(low_2), step(high_2)
    low, high, new_weight = lax.optimization_barrier((low_1, high_1, new_weight))
    spots = ((True, 0, 1), (True, BACK, 1), (False, 0, 1), (False, BACK, 1))
    new_weight = write_weight(place, held, (low, high, swap(low), swap(high)), spots, new_weight)
    low_2, high_2, low_3, new_weight = lax.optimization_barrier((low_2, high_2, low_3, new_weight))
    spots = ((True, 0, 2), (True, BACK, 2), (True, 0, 3))
    new_weight = write_weight(place, held, (low_2, high_2, low_3), spots, new_weight)
    low_2, high_2, low_3, high_3, new_weight = lax.optimization_barrier((low_2, high_2, low_3, high_3, new_weight))
    spots = ((False, 0, 2), (False, BACK, 2))
    new_weight = write_weight(place, held, (swap(low_2), swap(high_2)), spots, new_weight)
    spots = ((True, BACK, 3), (False, 0, 3), (False, BACK, 3))
    new_weight = write_weight(place, held, (high_3, swap(low_3), swap(high_3)), spots, new_weight)
    return (new_weight.T, *state)


def solution(mesh):
    fine = Mesh(mesh.devices.reshape(N_YH, N_Z, N_CORE, N_YL, N_X), AXES)
    blocks = P(DP + TENSOR)
    in_specs = (P(None, TENSOR), P(DP, None, TENSOR), blocks, blocks, blocks, blocks, P(), P(), P())
    out_specs = (P(None, TENSOR), blocks, blocks, blocks, blocks)
    return jax.shard_map(shards, mesh=fine, in_specs=in_specs, out_specs=out_specs, check_vma=False)
```
